32 devices in a mesh: groups: 2 (over x), space: 16 (over z, y, core).
Axes of the slice: x: 2, y: 2, z: 4, core: 2. Of those that a mesh axis runs over, the one named last changes fastest.
Arguments:
- grid_inputs: bfloat16 [227, 65536], P(None, ('groups', 'space')), parts along dimension 1, may hold values from -6 to 6
- grid_count: int32 [16], P('space'), may hold values from 1024 to 2048, as said below
- embed_in: bfloat16 [227, 512], replicated, may hold values from -0.375 to 0.375
- embed_out: bfloat16 [512, 512], replicated, may hold values from -0.25 to 0.25
- grid_gain: float32 [512], replicated, may hold values from 0.25 to 1.75
- g2m_values: bfloat16 [1024, 128, 128], P('space'), may hold values from -0.125 to 0.125
- g2m_src: int32 [1024], P('space'), may hold values from 0 to 15, as said below
- g2m_dst: int32 [1024], P('space'), may hold values from 0 to 63, as said below
- mesh_place: int32 [64], replicated, may hold values from 0 to 63, as said below
- node_in: bfloat16 [512, 512], replicated, may hold values from -0.25 to 0.25
- node_out: bfloat16 [512, 512], replicated, may hold values from -0.25 to 0.25
- node_gain: float32 [512], replicated, may hold values from 0.25 to 1.75
- recv_blocks: int32 [16, 4], P('space'), may hold values from 0 to 3, as said below
- mesh_values: bfloat16 [192, 128, 128], P('space'), may hold values from -0.3125 to 0.3125
- mesh_dst: int32 [192], P('space'), may hold values from 0 to 3, as said below
- mesh_src: int32 [192], P('space'), may hold values from 0 to 9, as said below
- proc_in: bfloat16 [512, 512], replicated, may hold values from -0.25 to 0.25
- proc_out: bfloat16 [512, 512], replicated, may hold values from -0.25 to 0.25
- proc_gain: float32 [512], replicated, may hold values from 0.25 to 1.75
Outputs:
- encoded: bfloat16 [16384, 512], P(('groups', 'space')), parts along dimension 0
- processed: bfloat16 [16384, 512], P(('groups', 'space')), parts along dimension 0
The draws below stay inside these ranges and needn't reach their ends.
There are 2 independent parts, one for each index of `groups`. The reference program is written for one: setup_inputs(seed, part) draws one part's arguments, and reference() takes and returns one part's arrays. A program takes and returns all parts, laid end to end along the dimension named above; an argument that names none is the same for every part. Nothing has to cross between parts.
Inputs may be any that keep to these rules, and one draw needn't show every extreme that they name: `grid_count`: live grid nodes of each latitude slab; a slab's rows from this count on are padding; some slab is full and some holds exactly 1024. `g2m_src`: each of a slab's 16 grid blocks is the source of exactly 4 of the slab's edge blocks. `g2m_dst`: of one slab's edge blocks at most 4 have targets held by any one partition (as mesh_place assigns them), and in every slab some partition holds exactly 4 of them. A permutation: mesh block g is block mesh_place[g] % 4 of partition mesh_place[g] // 4. `recv_blocks`: row p: the first 2 entries are distinct blocks of partition p - 1, the last 2 distinct blocks of partition p + 1 (partitions counted cyclically). `mesh_dst`: every block of a partition is the target of some of its edge blocks. `mesh_src`: code side * 4 + index: side 0 reads slot index of the lower list of recv_blocks, side 1 the partition's own block index, side 2 slot index of the upper list; slots lie below 2 and every slot of both lists is read by some edge block of the partition.
All inputs are finite; a program needn't handle non-finite values.
Results may differ from the reference program's by a relative error of at most 0.013.
Values may be sent and summed in bfloat16 or wider, within the bound.
No kernel may reach another device: no remote copies, remote signals or barrier semaphores. Data moves between devices by JAX's collectives and lax.ppermute only.
A program may use at most 128 MiB of HBM per device.

```python
import jax
import jax.numpy as jnp
from jax import lax

D = 512
C_IN = 227
BLK = 128
GB = 16
MB = 4
HC = 2
EG = 64
EM = 12
CAP = 4
G_DEV = 2048
GRID = 32768
MESH_BLOCKS = 64
MESH = 8192
EG_ALL = 1024
EM_ALL = 192
N_SPACE = 16


def block_places(key):
    return jax.random.permutation(jax.random.fold_in(key, 500), MESH_BLOCKS).astype(jnp.int32)


def draw_mesh_place(key, part):
    places = block_places(key)
    return places


def draw_g2m_dst(key, part):
    places = block_places(key)
    key = jax.random.fold_in(key, 12)
    key_shift, key_inner, key_order = jax.random.split(key, 3)
    at_position = jnp.argsort(places).astype(jnp.int32)
    last_place = places[MESH_BLOCKS - 1]
    first_place = places[0]
    shifts = jax.random.randint(key_shift, (N_SPACE,), 0, N_SPACE).astype(jnp.int32)
    shifts = shifts.at[0].set(last_place // MB).at[1].set(first_place // MB)
    inner = jax.random.randint(key_inner, (N_SPACE, EG), 0, MB).astype(jnp.int32)
    inner = inner.at[0, 0].set(last_place % MB).at[1, 0].set(first_place % MB)

    def ordering(row_key):
        others = jax.random.permutation(row_key, N_SPACE * CAP - CAP)[:EG - CAP] + CAP
        return jnp.concatenate([jnp.arange(CAP, dtype=jnp.int32), others.astype(jnp.int32)])
    orders = jax.vmap(ordering)(jax.random.split(key_order, N_SPACE))
    targets = (orders // CAP + shifts[:, None]) % N_SPACE
    positions = (targets * MB + inner).astype(jnp.int32)
    return at_position[positions].reshape(-1).astype(jnp.int32)


def draw_g2m_src(key, part):
    key = jax.random.fold_in(key, 13)
    pattern = jnp.arange(EG, dtype=jnp.int32) % GB
    rows = jax.vmap(lambda row_key: jax.random.permutation(row_key, pattern))(jax.random.split(key, N_SPACE))
    return rows.reshape(-1).astype(jnp.int32)


def draw_grid_count(key, part):
    key = jax.random.fold_in(key, 14)
    key_count, key_full = jax.random.split(key)
    counts = G_DEV // 2 + jax.random.randint(key_count, (N_SPACE,), 0, G_DEV // 2 + 1)
    fullest = jax.random.randint(key_full, (), 0, N_SPACE)
    counts = counts.at[fullest].set(G_DEV).at[(fullest + N_SPACE // 2) % N_SPACE].set(G_DEV // 2)
    return counts.astype(jnp.int32)


def draw_recv_blocks(key, part):
    key = jax.random.fold_in(key, 15)
    perms = jax.vmap(lambda row_key: jax.random.permutation(row_key, MB))(jax.random.split(key, N_SPACE * 2))
    perms = perms.reshape(N_SPACE, 2, MB)[:, :, :HC].astype(jnp.int32)
    offsets = jnp.zeros((N_SPACE, 2), jnp.int32)
    offsets = offsets.at[0, 0].set(MB - 1 - perms[0, 0, 0]).at[0, 1].set(MB - perms[0, 1, 0])
    lists = (perms + offsets[:, :, None]) % MB
    return lists.reshape(N_SPACE, 2 * HC).astype(jnp.int32)


def draw_mesh_dst(key, part):
    key = jax.random.fold_in(key, 16)
    random_rows = jax.random.randint(key, (N_SPACE, EM), 0, MB).astype(jnp.int32)
    positions = jnp.arange(EM, dtype=jnp.int32)
    targets = jnp.where(positions[None, :] < MB, positions[None, :] % MB, random_rows)
    return targets.reshape(-1).astype(jnp.int32)


def draw_mesh_src(key, part):
    key = jax.random.fold_in(key, 17)
    random_rows = jax.random.randint(key, (N_SPACE, EM), 0, 2 * MB).astype(jnp.int32)
    positions = jnp.arange(EM, dtype=jnp.int32)[None, :]
    own_codes = MB + random_rows % MB
    remote_step = positions - MB
    remote_codes = jnp.where(remote_step < HC, remote_step, 2 * MB + remote_step - HC)
    spare_codes = jnp.where(random_rows < HC, random_rows, jnp.where(random_rows < HC + MB, MB + random_rows - HC, 2 * MB + random_rows - HC - MB))
    codes = jnp.where(positions < MB, own_codes, jnp.where(positions < MB + 2 * HC, remote_codes, spare_codes))
    return codes.reshape(-1).astype(jnp.int32)


def block_scale(key, extent, shards, low, high):
    level = 1.0
    for axis_at, shards_of in shards:
        steps = jax.random.uniform(jax.random.fold_in(jax.random.fold_in(key, 6), axis_at), (shards_of,), jnp.float32, low / len(shards), high / len(shards))
        level = level * jnp.repeat(jnp.exp(steps), extent[axis_at] // shards_of).reshape((-1,) + (1,) * (len(extent) - 1 - axis_at))
    return level


def gaussian(key, shape, deviation, bound, cuts=(), held_as=jnp.bfloat16):
    level = block_scale(key, shape, cuts, -0.22, 0.18) if cuts else 1.0
    drawn = jax.random.normal(key, shape, jnp.float32) * deviation * level
    return jnp.minimum(jnp.maximum(drawn, -bound), bound).astype(held_as)


def setup_inputs(seed: int = 0, part: int = 0) -> dict:
    splits = jax.random.split(jax.random.key(seed), 20)
    part_keys = jax.random.split(jax.random.fold_in(splits[19], part), 20)
    return {
        "grid_inputs": gaussian(part_keys[0], (C_IN, GRID), 1.0, 6.0, ((1, 16),)),
        "grid_count": draw_grid_count(jax.random.fold_in(splits[19], 71), part),
        "embed_in": gaussian(splits[2], (C_IN, D), C_IN ** -0.5, 0.375),
        "embed_out": gaussian(splits[3], (D, D), D ** -0.5, 0.25),
        "grid_gain": jnp.clip(1.0 + 0.15 * jax.random.normal(splits[4], (D,), jnp.float32), 0.25, 1.75),
        "g2m_values": gaussian(splits[5], (EG_ALL, BLK, BLK), (BLK * EG // MB) ** -0.5, 0.125, ((0, 16),)),
        "g2m_src": draw_g2m_src(jax.random.fold_in(splits[19], 71), part),
        "g2m_dst": draw_g2m_dst(jax.random.fold_in(splits[19], 71), part),
        "mesh_place": draw_mesh_place(jax.random.fold_in(splits[19], 71), part),
        "node_in": gaussian(splits[9], (D, D), D ** -0.5, 0.25),
        "node_out": gaussian(splits[10], (D, D), D ** -0.5, 0.25),
        "node_gain": jnp.clip(1.0 + 0.15 * jax.random.normal(splits[11], (D,), jnp.float32), 0.25, 1.75),
        "recv_blocks": draw_recv_blocks(jax.random.fold_in(splits[19], 71), part),
        "mesh_values": gaussian(splits[13], (EM_ALL, BLK, BLK), (3 * BLK) ** -0.5, 0.3125, ((0, 16),)),
        "mesh_dst": draw_mesh_dst(jax.random.fold_in(splits[19], 71), part),
        "mesh_src": draw_mesh_src(jax.random.fold_in(splits[19], 71), part),
        "proc_in": gaussian(splits[16], (D, D), D ** -0.5, 0.25),
        "proc_out": gaussian(splits[17], (D, D), D ** -0.5, 0.25),
        "proc_gain": jnp.clip(1.0 + 0.15 * jax.random.normal(splits[18], (D,), jnp.float32), 0.25, 1.75),
    }


EPSILON = 1e-05

def normalize(values):
    average = lax.optimization_barrier(jnp.mean(values, axis=-1, keepdims=True))
    centred = values - average
    variance = lax.optimization_barrier(jnp.mean(centred * centred, axis=-1, keepdims=True))
    return centred * lax.rsqrt(variance + EPSILON)

def node_update(summed, weight_in, weight_out, gain):
    hidden = jax.nn.silu(jnp.dot(summed.astype(jnp.bfloat16), weight_in, preferred_element_type=jnp.float32)).astype(jnp.bfloat16)
    return (summed + gain * normalize(jnp.dot(hidden, weight_out, preferred_element_type=jnp.float32))).astype(jnp.bfloat16)

def block_product(values, sources):
    product = jnp.einsum('eij,ejd->eid', values.astype(jnp.float32), sources.astype(jnp.float32), precision=lax.Precision.HIGHEST)
    rounded = lax.optimization_barrier(product.astype(jnp.bfloat16))
    return rounded.astype(jnp.float32)

def reference(grid_inputs, grid_count, embed_in, embed_out, grid_gain, g2m_values, g2m_src, g2m_dst, mesh_place, node_in, node_out, node_gain, recv_blocks, mesh_values, mesh_dst, mesh_src, proc_in, proc_out, proc_gain):
    slab_list = jnp.arange(N_SPACE, dtype=jnp.int32)

    def embed_slab(slab_index):
        first_column = (slab_index * G_DEV).astype(jnp.int32)
        columns = lax.dynamic_slice_in_dim(grid_inputs, first_column, G_DEV, 1)
        embed_pre = lax.dot_general(columns, embed_in, (((0,), (0,)), ((), ())), preferred_element_type=jnp.float32)
        embed_hidden = jax.nn.silu(embed_pre).astype(jnp.bfloat16)
        embed_mixed = jnp.dot(embed_hidden, embed_out, preferred_element_type=jnp.float32)
        alive = jnp.arange(G_DEV, dtype=jnp.int32) < grid_count[slab_index]
        return jnp.where(alive[:, None], normalize(embed_mixed) * grid_gain, 0.0).astype(jnp.bfloat16)
    grid_latent = lax.map(embed_slab, slab_list)
    grid_blocks = grid_latent.reshape(N_SPACE * GB, BLK, D)

    def g2m_step(running, slab_index):
        first_edge = (slab_index * EG).astype(jnp.int32)
        values = lax.dynamic_slice_in_dim(g2m_values, first_edge, EG, 0)
        sources = (lax.dynamic_slice_in_dim(g2m_src, first_edge, EG, 0) + slab_index * GB).astype(jnp.int32)
        targets = lax.dynamic_slice_in_dim(g2m_dst, first_edge, EG, 0)
        edge_terms = block_product(values, grid_blocks[sources])
        return (running.at[targets].add(edge_terms), None)
    aggregated, _ = lax.scan(g2m_step, jnp.zeros((MESH_BLOCKS, BLK, D), jnp.float32), slab_list)
    mesh_sum = jnp.zeros_like(aggregated).at[mesh_place].set(aggregated).reshape(MESH, D)
    encoded = node_update(mesh_sum, node_in, node_out, node_gain)
    encoded_blocks = encoded.reshape(MESH_BLOCKS, BLK, D)

    def proc_step(running, part_index):
        first_edge = (part_index * EM).astype(jnp.int32)
        values = lax.dynamic_slice_in_dim(mesh_values, first_edge, EM, 0)
        source_codes = lax.dynamic_slice_in_dim(mesh_src, first_edge, EM, 0)
        targets = (lax.dynamic_slice_in_dim(mesh_dst, first_edge, EM, 0) + part_index * MB).astype(jnp.int32)
        side_code = source_codes // MB
        block_index = source_codes % MB
        list_row = recv_blocks[part_index]
        slot_index = jnp.minimum(jnp.where(side_code == 2, HC + block_index, block_index), 2 * HC - 1).astype(jnp.int32)
        remote_index = list_row[slot_index]
        held_index = jnp.where(side_code == 1, block_index, remote_index)
        owner_part = (part_index + side_code - 1 + N_SPACE) % N_SPACE
        sources = (owner_part * MB + held_index).astype(jnp.int32)
        edge_terms = block_product(values, encoded_blocks[sources])
        return (running.at[targets].add(edge_terms), None)
    message, _ = lax.scan(proc_step, jnp.zeros((MESH_BLOCKS, BLK, D), jnp.float32), slab_list)
    message = message.reshape(MESH, D)
    proc_hidden = jax.nn.silu(jnp.dot(message.astype(jnp.bfloat16), proc_in, preferred_element_type=jnp.float32)).astype(jnp.bfloat16)
    processed = (encoded.astype(jnp.float32) + proc_gain * normalize(jnp.dot(proc_hidden, proc_out, preferred_element_type=jnp.float32))).astype(jnp.bfloat16)
    return (encoded, processed)
```

```python
import functools

import jax
import jax.numpy as jnp
from jax import lax
from jax.experimental import pallas as pl
from jax.experimental.pallas import tpu as pltpu
from jax.sharding import PartitionSpec as P

EPSILON = 1e-05
LANES = 128
VMEM_BYTES = 56 * 1024 * 1024
VMEM = pl.BlockSpec(memory_space=pltpu.VMEM)
SMEM = pl.BlockSpec(memory_space=pltpu.SMEM)


def silu(values):
    half = 0.5 * values
    return half + half * jnp.tanh(half)


def normalize(values):
    average = jnp.mean(values, axis=-1, keepdims=True)
    centred = values - average
    variance = jnp.mean(centred * centred, axis=-1, keepdims=True)
    return centred * lax.rsqrt(variance + EPSILON)


def matmul(left, right):
    return jnp.dot(left, right, preferred_element_type=jnp.float32)


def transposed_matmul(left, right):
    return lax.dot_general(left, right, (((0,), (0,)), ((), ())), preferred_element_type=jnp.float32)


def add(left, right):
    return left.astype(jnp.float32) + right.astype(jnp.float32)


def place_of(step, order):
    place = 0
    for bit in order:
        place = place * 2 + ((step >> (bit - 1)) & 1)
    return place


def grid_kernel(
    tiles,
    held,
    capacity,
    src_ref,
    dst_ref,
    place_ref,
    count_ref,
    inputs_ref,
    embed_in_ref,
    embed_out_ref,
    gain_ref,
    values_ref,
    *refs,
):
    chunks = (len(refs) - 5) // 2
    mates, owns = refs[:chunks], refs[chunks : 2 * chunks]
    latent, edge_of, local_of, source_of, filled = refs[2 * chunks :]
    step = pl.program_id(0)
    tile_rows = inputs_ref.shape[1]
    rows = values_ref.shape[1]
    edges = src_ref.shape[0]

    @pl.when(step == 0)
    def _():
        me = lax.axis_index("space")

        def clear(slot, carry):
            filled[slot] = 0
            return carry

        lax.fori_loop(0, edges // capacity, clear, 0)

        def sort(edge, carry):
            position = place_ref[dst_ref[edge]]
            slot = lax.div(position, held) ^ me
            at = slot * capacity + filled[slot]
            edge_of[at] = edge
            local_of[at] = lax.rem(position, held)
            source_of[at] = src_ref[edge]
            filled[slot] = filled[slot] + 1
            return carry

        lax.fori_loop(0, edges, sort, 0)

    @pl.when(step < tiles)
    def _():
        hidden = silu(transposed_matmul(inputs_ref[...], embed_in_ref[...])).astype(jnp.bfloat16)
        scaled = normalize(matmul(hidden, embed_out_ref[...])) * gain_ref[...]
        first = pl.multiple_of(step * tile_rows, tile_rows)
        row = first + lax.broadcasted_iota(jnp.int32, (tile_rows, 1), 0)
        latent[pl.ds(first, tile_rows), :] = jnp.where(row < count_ref[0], scaled, 0.0).astype(jnp.bfloat16)

    @pl.when(step >= tiles)
    def _():
        for side, outs in ((0, owns), (1, mates)):
            first = (2 * (step - tiles) + side) * capacity
            operator = []
            sources = []
            for index in range(capacity):
                values = values_ref[edge_of[first + index]]
                local = local_of[first + index]
                zeros = jnp.zeros_like(values)
                operator.append(
                    jnp.concatenate([jnp.where(local == block, values, zeros) for block in range(held)], axis=0)
                )
                start = pl.multiple_of(source_of[first + index] * rows, rows)
                sources.append(latent[pl.ds(start, rows), :])
            summed = matmul(jnp.concatenate(operator, axis=1), jnp.concatenate(sources, axis=0))
            width = summed.shape[1] // chunks
            for chunk, out in enumerate(outs):
                out[...] = summed[:, chunk * width : (chunk + 1) * width].astype(jnp.bfloat16)


def slab_sums(
    grid_inputs, grid_count, embed_in, embed_out, grid_gain, g2m_values, g2m_src, g2m_dst, mesh_place, partitions, orders
):
    tile_rows = 256
    channels_in, slab_rows = grid_inputs.shape
    channels = embed_out.shape[1]
    edges, rows, _ = g2m_values.shape
    held = mesh_place.shape[0] // partitions
    capacity = edges // partitions
    tiles = slab_rows // tile_rows
    pairs = partitions // 2
    width = channels // len(orders)

    def out_spec(order):
        return pl.BlockSpec(
            (held * rows, width), lambda step: (place_of(jnp.maximum(step - tiles, 0), order), 0)
        )

    whole = lambda shape: pl.BlockSpec(shape, lambda step: (0,) * len(shape))
    out_specs = [out_spec(order) for order in orders] * 2
    return pl.pallas_call(
        functools.partial(grid_kernel, tiles, held, capacity),
        grid=(tiles + pairs,),
        in_specs=[
            SMEM,
            SMEM,
            SMEM,
            SMEM,
            pl.BlockSpec((channels_in, tile_rows), lambda step: (0, jnp.minimum(step, tiles - 1))),
            whole(embed_in.shape),
            whole(embed_out.shape),
            whole((1, channels)),
            whole(g2m_values.shape),
        ],
        out_specs=out_specs,
        out_shape=[jax.ShapeDtypeStruct((pairs * held * rows, width), jnp.bfloat16)] * len(out_specs),
        scratch_shapes=[
            pltpu.VMEM((slab_rows, channels), jnp.bfloat16),
            pltpu.SMEM((edges,), jnp.int32),
            pltpu.SMEM((edges,), jnp.int32),
            pltpu.SMEM((edges,), jnp.int32),
            pltpu.SMEM((partitions,), jnp.int32),
        ],
        compiler_params=pltpu.CompilerParams(vmem_limit_bytes=VMEM_BYTES),
        name="grid_to_mesh",
    )(g2m_src, g2m_dst, mesh_place, grid_count, grid_inputs, embed_in, embed_out, grid_gain.reshape(1, -1), g2m_values)


def exchange(cells, bit):
    count = lax.axis_size("space")
    return lax.ppermute(cells, "space", [(i, i ^ (1 << bit)) for i in range(count)])


def reduce_chunks(mates, owns, orders):
    arrived = [exchange(mate, 0) for mate in mates]
    kept = list(owns)
    for stage in range(len(orders[0])):
        for chunk, order in enumerate(orders):
            half = kept[chunk].shape[0] // 2
            send = add(arrived[chunk][half:], kept[chunk][half:]).astype(jnp.bfloat16)
            kept[chunk] = add(arrived[chunk][:half], kept[chunk][:half]).astype(jnp.bfloat16)
            arrived[chunk] = exchange(send, order[stage])
    return arrived, kept


def node_kernel(parts, reads, rows, wanted_ref, *refs):
    summands = refs[:parts]
    node_in_ref, node_out_ref, gain_ref, encoded_ref, upward_ref, downward_ref = refs[parts:]
    if parts == 1:
        summed = summands[0][...]
    else:
        chunks = parts // 2
        summed = jnp.concatenate(
            [add(summands[chunk][...], summands[chunks + chunk][...]) for chunk in range(chunks)], axis=1
        )
    hidden = silu(matmul(summed.astype(jnp.bfloat16), node_in_ref[...])).astype(jnp.bfloat16)
    encoded_ref[...] = (summed + gain_ref[...] * normalize(matmul(hidden, node_out_ref[...]))).astype(jnp.bfloat16)
    for index in range(reads):
        for first, out in ((0, upward_ref), (reads, downward_ref)):
            start = pl.multiple_of(wanted_ref[first + index] * rows, rows)
            out[index * rows : (index + 1) * rows, :] = encoded_ref[pl.ds(start, rows), :]


def encode(summands, node_in, node_out, node_gain, wanted, held, rows):
    channels = node_in.shape[0]
    reads = wanted.shape[0] // 2
    return pl.pallas_call(
        functools.partial(node_kernel, len(summands), reads, rows),
        in_specs=[SMEM] + [VMEM] * (len(summands) + 3),
        out_specs=[VMEM] * 3,
        out_shape=[
            jax.ShapeDtypeStruct((held * rows, channels), jnp.bfloat16),
            jax.ShapeDtypeStruct((reads * rows, channels), jnp.bfloat16),
            jax.ShapeDtypeStruct((reads * rows, channels), jnp.bfloat16),
        ],
        compiler_params=pltpu.CompilerParams(vmem_limit_bytes=VMEM_BYTES),
        name="node_update",
    )(wanted, *summands, node_in, node_out, node_gain.reshape(1, -1))


def process_kernel(
    held,
    reads,
    dst_ref,
    src_ref,
    encoded_ref,
    lower_ref,
    upper_ref,
    values_ref,
    proc_in_ref,
    proc_out_ref,
    gain_ref,
    processed_ref,
    frame,
):
    edges, rows, _ = values_ref.shape
    frame[: reads * rows, :] = lower_ref[...]
    frame[held * rows : 2 * held * rows, :] = encoded_ref[...]
    frame[2 * held * rows : (2 * held + reads) * rows, :] = upper_ref[...]
    operator = []
    sources = []
    for edge in range(edges):
        values = values_ref[edge]
        zeros = jnp.zeros_like(values)
        local = dst_ref[edge]
        operator.append(
            jnp.concatenate([jnp.where(local == block, values, zeros) for block in range(held)], axis=0)
        )
        start = pl.multiple_of(src_ref[edge] * rows, rows)
        sources.append(frame[pl.ds(start, rows), :])
    message = matmul(jnp.concatenate(operator, axis=1), jnp.concatenate(sources, axis=0))
    hidden = silu(matmul(message.astype(jnp.bfloat16), proc_in_ref[...])).astype(jnp.bfloat16)
    update = gain_ref[...] * normalize(matmul(hidden, proc_out_ref[...]))
    processed_ref[...] = (encoded_ref[...].astype(jnp.float32) + update).astype(jnp.bfloat16)


def process(encoded, lower, upper, mesh_values, mesh_dst, mesh_src, proc_in, proc_out, proc_gain, held, reads):
    rows = mesh_values.shape[1]
    return pl.pallas_call(
        functools.partial(process_kernel, held, reads),
        in_specs=[SMEM] * 2 + [VMEM] * 7,
        out_specs=VMEM,
        out_shape=jax.ShapeDtypeStruct(encoded.shape, jnp.bfloat16),
        scratch_shapes=[pltpu.VMEM(((2 * held + reads) * rows, encoded.shape[1]), jnp.bfloat16)],
        compiler_params=pltpu.CompilerParams(vmem_limit_bytes=VMEM_BYTES),
        name="process",
    )(mesh_dst, mesh_src, encoded, lower, upper, mesh_values, proc_in, proc_out, proc_gain.reshape(1, -1))


def lookup(table, wanted):
    matches = wanted[:, None] == jnp.arange(table.shape[0], dtype=jnp.int32)[None, :]
    return jnp.sum(jnp.where(matches, table[None, :], 0), axis=1)


def routed_sum(
    grid_inputs, grid_count, embed_in, embed_out, grid_gain, g2m_values, g2m_src, g2m_dst, mesh_place, partitions
):
    slab_rows = grid_inputs.shape[1]
    edge_count, block_rows, _ = g2m_values.shape
    channels = embed_out.shape[1]
    held = mesh_place.shape[0] // partitions
    capacity = max(1, (edge_count + partitions - 1) // partitions)
    slot_count = partitions * capacity
    hidden = jax.nn.silu(transposed_matmul(grid_inputs, embed_in)).astype(jnp.bfloat16)
    alive = lax.iota(jnp.int32, slab_rows) < grid_count[0]
    latent = jnp.where(alive[:, None], normalize(matmul(hidden, embed_out)) * grid_gain, 0.0).astype(jnp.bfloat16)
    positions = lookup(mesh_place, g2m_dst)
    targets = positions // held
    ranking = jnp.sum(jnp.tril(targets[:, None] == targets[None, :], -1), axis=1)
    slot_index = targets * capacity + ranking
    labels = jnp.full((slot_count,), -1, jnp.int32).at[slot_index].set(positions % held)
    sources = latent.reshape(slab_rows // block_rows, block_rows, channels)[g2m_src]
    terms = jnp.einsum("eij,ejd->eid", g2m_values, sources, preferred_element_type=jnp.float32).astype(jnp.bfloat16)
    outgoing = jnp.zeros((slot_count, block_rows, channels), jnp.bfloat16).at[slot_index].set(terms)
    arrived = lax.all_to_all(outgoing, "space", split_axis=0, concat_axis=0, tiled=True)
    arrived_labels = lax.all_to_all(labels, "space", split_axis=0, concat_axis=0, tiled=True)
    selector = (arrived_labels[None, :] == jnp.arange(held, dtype=jnp.int32)[:, None]).astype(jnp.bfloat16)
    return matmul(selector, arrived.reshape(slot_count, -1)).reshape(held * block_rows, channels)


def shards(
    grid_inputs,
    grid_count,
    embed_in,
    embed_out,
    grid_gain,
    g2m_values,
    g2m_src,
    g2m_dst,
    mesh_place,
    node_in,
    node_out,
    node_gain,
    recv_blocks,
    mesh_values,
    mesh_dst,
    mesh_src,
    proc_in,
    proc_out,
    proc_gain,
):
    partitions = lax.axis_size("space")
    edges, rows, _ = g2m_values.shape
    mesh_blocks = mesh_place.shape[0]
    held = mesh_blocks // partitions
    reads = recv_blocks.shape[1] // 2
    bits = partitions.bit_length() - 1
    upward = [(i, (i + 1) % partitions) for i in range(partitions)]
    downward = [((i + 1) % partitions, i) for i in range(partitions)]
    grid_args = (grid_inputs, grid_count, embed_in, embed_out, grid_gain, g2m_values, g2m_src, g2m_dst, mesh_place)
    if partitions == 1 << bits and bits >= 3 and edges % partitions == 0 and edges >= mesh_blocks:
        near_first = tuple(range(1, bits))
        far_first = (2, 1) + tuple(range(3, bits))
        orders = [far_first, near_first, far_first, near_first]
        sums = slab_sums(*grid_args, partitions, orders)
        arrived, kept = reduce_chunks(sums[: len(orders)], sums[len(orders) :], orders)
        summands = arrived + kept
    else:
        summands = [routed_sum(*grid_args, partitions)]
    wanted = jnp.concatenate(
        [
            lax.ppermute(recv_blocks[0, :reads], "space", downward),
            lax.ppermute(recv_blocks[0, reads:], "space", upward),
        ]
    )
    encoded, to_upper, to_lower = encode(summands, node_in, node_out, node_gain, wanted, held, rows)
    lower = lax.ppermute(to_upper, "space", upward)
    upper = lax.ppermute(to_lower, "space", downward)
    processed = process(
        encoded, lower, upper, mesh_values, mesh_dst, mesh_src, proc_in, proc_out, proc_gain, held, reads
    )
    return (encoded, processed)


def solution(mesh):
    return jax.shard_map(
        shards,
        mesh=mesh,
        in_specs=(
            P(None, ("groups", "space")),
            P("space"),
            P(),
            P(),
            P(),
            P("space", None, None),
            P("space"),
            P("space"),
            P(),
            P(),
            P(),
            P(),
            P("space", None),
            P("space", None, None),
            P("space"),
            P("space"),
            P(),
            P(),
            P(),
        ),
        out_specs=(P(("groups", "space"), None), P(("groups", "space"), None)),
        check_vma=False,
    )
```

```python
import functools

import jax
import jax.numpy as jnp
from jax import lax
from jax.experimental import pallas as pl
from jax.experimental.pallas import tpu as pltpu
from jax.sharding import PartitionSpec as P

EPSILON = 1e-05
ORDERS = ((1, 3, 2), (1, 2, 3), (3, 1, 2), (2, 1, 3), (2, 1, 3))
SHARES = (2, 2, 2, 1, 1)
TURNS = (0, 1, 2, 3, 4, 0, 3, 1, 2, 4, 3, 2, 4, 0, 1)
VMEM_BYTES = 24 * 1024 * 1024
GRID_VMEM_BYTES = 60 * 1024 * 1024
VMEM = pl.BlockSpec(memory_space=pltpu.VMEM)
SMEM = pl.BlockSpec(memory_space=pltpu.SMEM)
ANY = pl.BlockSpec(memory_space=pl.ANY)


def silu(values):
    half = 0.5 * values
    return half + half * jnp.tanh(half)


def normalize(values):
    average = jnp.mean(values, axis=-1, keepdims=True)
    centred = values - average
    variance = jnp.mean(centred * centred, axis=-1, keepdims=True)
    return centred * lax.rsqrt(variance + EPSILON)


def matmul(left, right):
    return jnp.dot(left, right, preferred_element_type=jnp.float32)


def transposed_matmul(left, right):
    return lax.dot_general(left, right, (((0,), (0,)), ((), ())), preferred_element_type=jnp.float32)


def add(left, right):
    return left.astype(jnp.float32) + right.astype(jnp.float32)


def place_of(step, order):
    place = 0
    for bit in order:
        place = place * 2 + ((step >> (bit - 1)) & 1)
    return place


def grid_kernel(
    held,
    capacity,
    orders,
    cuts,
    tile_rows,
    src_ref,
    dst_ref,
    place_ref,
    count_ref,
    gain_ref,
    inputs_hbm,
    embed_in_hbm,
    embed_out_hbm,
    values_hbm,
    *refs,
):
    chunks = len(orders)
    outs = (refs[chunks : 2 * chunks], refs[:chunks])
    (
        inputs_ref,
        embed_in_ref,
        embed_out_ref,
        values_ref,
        latent,
        staged,
        edge_of,
        filled,
        crowded_of,
        crowded,
        load_sems,
        store_sems,
    ) = refs[2 * chunks :]
    rows = values_ref.shape[1]
    edges = src_ref.shape[0]
    slots = edges // capacity
    pairs = slots // 2
    loads = [
        pltpu.make_async_copy(source, target, load_sems.at[index])
        for index, (source, target) in enumerate(
            (
                (inputs_hbm, inputs_ref),
                (embed_in_hbm, embed_in_ref),
                (embed_out_hbm, embed_out_ref),
                (values_hbm, values_ref),
            )
        )
    ]
    for load in loads:
        load.start()

    me = lax.axis_index("space")

    def clear(bin_, carry):
        filled[bin_] = 0
        for index in range(2):
            edge_of[bin_ * capacity + index] = 0
        return carry

    def clear_pair(pair, carry):
        crowded[pair] = 0
        return carry

    lax.fori_loop(0, slots * held, clear, 0)
    lax.fori_loop(0, pairs, clear_pair, 0)

    def sort(edge, carry):
        bin_ = place_ref[dst_ref[edge]] ^ (me * held)
        count = filled[bin_]
        edge_of[bin_ * capacity + count] = edge
        filled[bin_] = count + 1

        @pl.when(count == 2)
        def _():
            pair = lax.div(bin_, 2 * held)
            seen = crowded[pair]
            crowded_of[pair * 2 * held + seen] = bin_
            crowded[pair] = seen + 1

        return carry

    lax.fori_loop(0, edges, sort, 0)

    for load in loads[:3]:
        load.wait()

    def embed(tile, carry):
        first = pl.multiple_of(tile * tile_rows, tile_rows)
        columns = inputs_ref[:, pl.ds(first, tile_rows)]
        hidden = silu(transposed_matmul(columns, embed_in_ref[...])).astype(jnp.bfloat16)
        scaled = normalize(matmul(hidden, embed_out_ref[...])) * gain_ref[...]
        row = first + lax.broadcasted_iota(jnp.int32, (tile_rows, 1), 0)
        latent[pl.ds(first, tile_rows), :] = jnp.where(row < count_ref[0], scaled, 0.0).astype(jnp.bfloat16)
        return carry

    lax.fori_loop(0, latent.shape[0] // tile_rows, embed, 0)
    loads[3].wait()

    def stores(pair):
        copies = []
        for side in range(2):
            first = 0
            for chunk, order in enumerate(orders):
                count = held * cuts[chunk]
                start = pl.multiple_of(place_of(pair, order) * count, count)
                copies.append(
                    pltpu.make_async_copy(
                        staged.at[pair, side, pl.ds(first, count), :],
                        outs[side][chunk].at[pl.ds(start, count), :],
                        store_sems.at[pair, side, chunk],
                    )
                )
                first += count
        return copies

    def product(bin_, first, count):
        operator = []
        sources = []
        for index in range(first, first + 2):
            edge = jnp.where(count > index, edge_of[bin_ * capacity + index], 0)
            values = values_ref[edge]
            operator.append(jnp.where(count > index, values, jnp.zeros_like(values)))
            start = pl.multiple_of(src_ref[edge] * rows, rows)
            sources.append(latent[pl.ds(start, rows), :])
        return matmul(jnp.concatenate(operator, axis=1), jnp.concatenate(sources, axis=0))

    def stage(pair, side, block, summed):
        top = 0
        for cut in cuts:
            first = pl.multiple_of(top * held + block * cut, 16)
            staged[pair, side, pl.ds(first, cut), :] = summed[top : top + cut].astype(jnp.bfloat16)
            top += cut

    def multiply(pair, carry):
        for side in range(2):
            for block in range(held):
                bin_ = (2 * pair + side) * held + block
                stage(pair, side, block, product(bin_, 0, filled[bin_]))

        def revisit(index, carry):
            bin_ = crowded_of[pair * 2 * held + index]
            count = filled[bin_]
            summed = product(bin_, 0, count)
            for first in range(2, capacity, 2):
                summed = summed + product(bin_, first, count)
            stage(pair, lax.div(lax.rem(bin_, 2 * held), held), lax.rem(bin_, held), summed)
            return carry

        lax.fori_loop(0, crowded[pair], revisit, 0)
        for copy in stores(pair):
            copy.start()
        return carry

    lax.fori_loop(0, pairs, multiply, 0)

    def finish(pair, carry):
        for copy in stores(pair):
            copy.wait()
        return carry

    lax.fori_loop(0, pairs, finish, 0)


def slab_sums(
    grid_inputs,
    grid_count,
    embed_in,
    embed_out,
    grid_gain,
    g2m_values,
    g2m_src,
    g2m_dst,
    mesh_place,
    partitions,
    orders,
    cuts,
):
    slab_rows = grid_inputs.shape[1]
    channels = embed_out.shape[1]
    edges, rows, _ = g2m_values.shape
    held = mesh_place.shape[0] // partitions
    capacity = edges // partitions
    pairs = partitions // 2
    shapes = [jax.ShapeDtypeStruct((pairs * held * cut, channels), jnp.bfloat16) for cut in cuts]
    return pl.pallas_call(
        functools.partial(grid_kernel, held, capacity, orders, cuts, min(512, slab_rows)),
        in_specs=[SMEM] * 4 + [VMEM] + [ANY] * 4,
        out_specs=[ANY] * (2 * len(cuts)),
        out_shape=shapes * 2,
        scratch_shapes=[
            pltpu.VMEM(grid_inputs.shape, jnp.bfloat16),
            pltpu.VMEM(embed_in.shape, jnp.bfloat16),
            pltpu.VMEM(embed_out.shape, jnp.bfloat16),
            pltpu.VMEM(g2m_values.shape, jnp.bfloat16),
            pltpu.VMEM((slab_rows, channels), jnp.bfloat16),
            pltpu.VMEM((pairs, 2, held * rows, channels), jnp.bfloat16),
            pltpu.SMEM((partitions * held * capacity,), jnp.int32),
            pltpu.SMEM((partitions * held,), jnp.int32),
            pltpu.SMEM((partitions * held,), jnp.int32),
            pltpu.SMEM((pairs,), jnp.int32),
            pltpu.SemaphoreType.DMA((4,)),
            pltpu.SemaphoreType.DMA((pairs, 2, len(cuts))),
        ],
        compiler_params=pltpu.CompilerParams(vmem_limit_bytes=GRID_VMEM_BYTES),
        name="grid_to_mesh",
    )(
        g2m_src,
        g2m_dst,
        mesh_place,
        grid_count,
        grid_gain.reshape(1, -1),
        grid_inputs,
        embed_in,
        embed_out,
        g2m_values,
    )


def exchange(cells, bit):
    count = lax.axis_size("space")
    return lax.ppermute(cells, "space", [(i, i ^ (1 << bit)) for i in range(count)])


def reduce_chunks(mates, owns, orders, turns, lists):
    arrived = [exchange(mate, 0) for mate in mates]
    kept = list(owns)
    made = [0] * len(orders)
    for turn, chunk in enumerate(turns):
        received = arrived[chunk]
        if turn == len(orders):
            received, _, lists = lax.optimization_barrier((received, previous, lists))
        elif turn > 0:
            received, _ = lax.optimization_barrier((received, previous))
        half = kept[chunk].shape[0] // 2
        previous = add(received[half:], kept[chunk][half:]).astype(jnp.bfloat16)
        kept[chunk] = add(received[:half], kept[chunk][:half]).astype(jnp.bfloat16)
        arrived[chunk] = exchange(previous, orders[chunk][made[chunk]])
        made[chunk] += 1
    return arrived, kept, lists


def node_kernel(parts, reads, rows, mate_list_ref, other_list_ref, *refs):
    summands = refs[:parts]
    node_in_ref, node_out_ref, gain_ref, encoded_ref, to_mate_ref, to_other_ref = refs[parts:]
    if parts == 1:
        summed = summands[0][...]
    else:
        chunks = parts // 2
        held = encoded_ref.shape[0] // rows
        pieces = [add(summands[chunk][...], summands[chunks + chunk][...]) for chunk in range(chunks)]
        cuts = [piece.shape[0] // held for piece in pieces]
        summed = jnp.concatenate(
            [
                piece[block * cut : (block + 1) * cut]
                for block in range(held)
                for piece, cut in zip(pieces, cuts)
            ],
            axis=0,
        )
    hidden = silu(matmul(summed.astype(jnp.bfloat16), node_in_ref[...])).astype(jnp.bfloat16)
    encoded_ref[...] = (summed + gain_ref[...] * normalize(matmul(hidden, node_out_ref[...]))).astype(jnp.bfloat16)
    odd = lax.rem(lax.axis_index("space"), 2)
    for index in range(reads):
        for wanted_ref, first, out in (
            (mate_list_ref, odd * reads, to_mate_ref),
            (other_list_ref, (1 - odd) * reads, to_other_ref),
        ):
            start = pl.multiple_of(wanted_ref[0, first + index] * rows, rows)
            out[index * rows : (index + 1) * rows, :] = encoded_ref[pl.ds(start, rows), :]


def encode(summands, node_in, node_out, node_gain, lists, held, rows):
    channels = node_in.shape[0]
    reads = lists[0].shape[1] // 2
    return pl.pallas_call(
        functools.partial(node_kernel, len(summands), reads, rows),
        in_specs=[SMEM] * 2 + [VMEM] * (len(summands) + 3),
        out_specs=[VMEM] * 3,
        out_shape=[
            jax.ShapeDtypeStruct((held * rows, channels), jnp.bfloat16),
            jax.ShapeDtypeStruct((reads * rows, channels), jnp.bfloat16),
            jax.ShapeDtypeStruct((reads * rows, channels), jnp.bfloat16),
        ],
        compiler_params=pltpu.CompilerParams(vmem_limit_bytes=VMEM_BYTES),
        name="node_update",
    )(*lists, *summands, node_in, node_out, node_gain.reshape(1, -1))


def process_kernel(
    held,
    reads,
    dst_ref,
    src_ref,
    encoded_ref,
    mate_ref,
    other_ref,
    values_ref,
    proc_in_ref,
    proc_out_ref,
    gain_ref,
    processed_ref,
    frame,
):
    edges, rows, _ = values_ref.shape
    frame[: reads * rows, :] = mate_ref[...]
    frame[reads * rows : 2 * reads * rows, :] = other_ref[...]
    frame[2 * reads * rows :, :] = encoded_ref[...]
    odd = lax.rem(lax.axis_index("space"), 2)
    operator = []
    sources = []
    for edge in range(edges):
        values = values_ref[edge]
        zeros = jnp.zeros_like(values)
        local = dst_ref[edge]
        operator.append(
            jnp.concatenate([jnp.where(local == block, values, zeros) for block in range(held)], axis=0)
        )
        side = lax.div(src_ref[edge], held)
        index = lax.rem(src_ref[edge], held)
        across = (odd + lax.div(side, 2) + 1) & 1
        at = jnp.where(side == 1, 2 * reads, across * reads) + index
        start = pl.multiple_of(at * rows, rows)
        sources.append(frame[pl.ds(start, rows), :])
    message = matmul(jnp.concatenate(operator, axis=1), jnp.concatenate(sources, axis=0))
    hidden = silu(matmul(message.astype(jnp.bfloat16), proc_in_ref[...])).astype(jnp.bfloat16)
    update = gain_ref[...] * normalize(matmul(hidden, proc_out_ref[...]))
    processed_ref[...] = (encoded_ref[...].astype(jnp.float32) + update).astype(jnp.bfloat16)


def process(encoded, from_mate, from_other, mesh_values, mesh_dst, mesh_src, proc_in, proc_out, proc_gain, held, reads):
    rows = mesh_values.shape[1]
    return pl.pallas_call(
        functools.partial(process_kernel, held, reads),
        in_specs=[SMEM] * 2 + [VMEM] * 7,
        out_specs=VMEM,
        out_shape=jax.ShapeDtypeStruct(encoded.shape, jnp.bfloat16),
        scratch_shapes=[pltpu.VMEM(((2 * reads + held) * rows, encoded.shape[1]), jnp.bfloat16)],
        compiler_params=pltpu.CompilerParams(vmem_limit_bytes=VMEM_BYTES),
        name="process",
    )(mesh_dst, mesh_src, encoded, from_mate, from_other, mesh_values, proc_in, proc_out, proc_gain.reshape(1, -1))


def lookup(table, wanted):
    matches = wanted[:, None] == jnp.arange(table.shape[0], dtype=jnp.int32)[None, :]
    return jnp.sum(jnp.where(matches, table[None, :], 0), axis=1)


def routed_sum(
    grid_inputs, grid_count, embed_in, embed_out, grid_gain, g2m_values, g2m_src, g2m_dst, mesh_place, partitions
):
    slab_rows = grid_inputs.shape[1]
    edge_count, block_rows, _ = g2m_values.shape
    channels = embed_out.shape[1]
    held = mesh_place.shape[0] // partitions
    capacity = max(1, (edge_count + partitions - 1) // partitions)
    slot_count = partitions * capacity
    hidden = jax.nn.silu(transposed_matmul(grid_inputs, embed_in)).astype(jnp.bfloat16)
    alive = lax.iota(jnp.int32, slab_rows) < grid_count[0]
    latent = jnp.where(alive[:, None], normalize(matmul(hidden, embed_out)) * grid_gain, 0.0).astype(jnp.bfloat16)
    positions = lookup(mesh_place, g2m_dst)
    targets = positions // held
    ranking = jnp.sum(jnp.tril(targets[:, None] == targets[None, :], -1), axis=1)
    slot_index = targets * capacity + ranking
    labels = jnp.full((slot_count,), -1, jnp.int32).at[slot_index].set(positions % held)
    sources = latent.reshape(slab_rows // block_rows, block_rows, channels)[g2m_src]
    terms = jnp.einsum("eij,ejd->eid", g2m_values, sources, preferred_element_type=jnp.float32).astype(jnp.bfloat16)
    outgoing = jnp.zeros((slot_count, block_rows, channels), jnp.bfloat16).at[slot_index].set(terms)
    arrived = lax.all_to_all(outgoing, "space", split_axis=0, concat_axis=0, tiled=True)
    arrived_labels = lax.all_to_all(labels, "space", split_axis=0, concat_axis=0, tiled=True)
    selector = (arrived_labels[None, :] == jnp.arange(held, dtype=jnp.int32)[:, None]).astype(jnp.bfloat16)
    return matmul(selector, arrived.reshape(slot_count, -1)).reshape(held * block_rows, channels)


def shards(
    grid_inputs,
    grid_count,
    embed_in,
    embed_out,
    grid_gain,
    g2m_values,
    g2m_src,
    g2m_dst,
    mesh_place,
    node_in,
    node_out,
    node_gain,
    recv_blocks,
    mesh_values,
    mesh_dst,
    mesh_src,
    proc_in,
    proc_out,
    proc_gain,
):
    partitions = lax.axis_size("space")
    edges, rows, _ = g2m_values.shape
    mesh_blocks = mesh_place.shape[0]
    held = mesh_blocks // partitions
    reads = recv_blocks.shape[1] // 2
    mates = [(i, i ^ 1) for i in range(partitions)]
    others = [(i, (i + 1 if i % 2 else i - 1) % partitions) for i in range(partitions)]
    lists = (lax.ppermute(recv_blocks, "space", mates), lax.ppermute(recv_blocks, "space", others))
    grid_args = (grid_inputs, grid_count, embed_in, embed_out, grid_gain, g2m_values, g2m_src, g2m_dst, mesh_place)
    if partitions == 1 << (1 + len(ORDERS[0])) and edges % partitions == 0 and edges >= mesh_blocks:
        cuts = [share * rows // sum(SHARES) for share in SHARES]
        sums = slab_sums(*grid_args, partitions, ORDERS, cuts)
        arrived, kept, lists = reduce_chunks(sums[: len(cuts)], sums[len(cuts) :], ORDERS, TURNS, lists)
        summands = arrived + kept
    else:
        summands = [routed_sum(*grid_args, partitions)]
    encoded, to_mate, to_other = encode(summands, node_in, node_out, node_gain, lists, held, rows)
    from_other = lax.ppermute(to_other, "space", others)
    from_mate = lax.ppermute(to_mate, "space", mates)
    processed = process(
        encoded, from_mate, from_other, mesh_values, mesh_dst, mesh_src, proc_in, proc_out, proc_gain, held, reads
    )
    return (encoded, processed)


def solution(mesh):
    return jax.shard_map(
        shards,
        mesh=mesh,
        in_specs=(
            P(None, ("groups", "space")),
            P("space"),
            P(),
            P(),
            P(),
            P("space", None, None),
            P("space"),
            P("space"),
            P(),
            P(),
            P(),
            P(),
            P("space", None),
            P("space", None, None),
            P("space"),
            P("space"),
            P(),
            P(),
            P(),
        ),
        out_specs=(P(("groups", "space"), None), P(("groups", "space"), None)),
        check_vma=False,
    )
```

```python
import functools

import jax
import jax.numpy as jnp
from jax import lax
from jax.experimental import pallas as pl
from jax.experimental.pallas import tpu as pltpu
from jax.sharding import PartitionSpec as P

EPSILON = 1e-05
ORDERS = ((1, 3, 2), (1, 2, 3), (3, 1, 2), (2, 1, 3), (2, 1, 3))
SHARES = (2, 2, 2, 1, 1)
TURNS = (0, 1, 2, 3, 4, 0, 3, 1, 2, 4, 3, 2, 4, 0, 1)
VMEM_BYTES = 24 * 1024 * 1024
GRID_VMEM_BYTES = 60 * 1024 * 1024
VMEM = pl.BlockSpec(memory_space=pltpu.VMEM)
SMEM = pl.BlockSpec(memory_space=pltpu.SMEM)
ANY = pl.BlockSpec(memory_space=pl.ANY)


def silu(values):
    half = 0.5 * values
    return half + half * jnp.tanh(half)


def normalize(values):
    average = jnp.mean(values, axis=-1, keepdims=True)
    centred = values - average
    variance = jnp.mean(centred * centred, axis=-1, keepdims=True)
    return centred * lax.rsqrt(variance + EPSILON)


def matmul(left, right):
    return jnp.dot(left, right, preferred_element_type=jnp.float32)


def transposed_matmul(left, right):
    return lax.dot_general(left, right, (((0,), (0,)), ((), ())), preferred_element_type=jnp.float32)


def add(left, right):
    return left.astype(jnp.float32) + right.astype(jnp.float32)


def place_of(step, order):
    place = 0
    for bit in order:
        place = place * 2 + ((step >> (bit - 1)) & 1)
    return place


def grid_kernel(
    held,
    capacity,
    orders,
    cuts,
    tile_rows,
    src_ref,
    dst_ref,
    place_ref,
    count_ref,
    gain_ref,
    inputs_hbm,
    embed_in_hbm,
    embed_out_hbm,
    values_hbm,
    *refs,
):
    chunks = len(orders)
    outs = (refs[chunks : 2 * chunks], refs[:chunks])
    (
        inputs_ref,
        embed_in_ref,
        embed_out_ref,
        values_ref,
        latent,
        staged,
        edge_of,
        filled,
        crowded_of,
        crowded,
        load_sems,
        store_sems,
    ) = refs[2 * chunks :]
    rows = values_ref.shape[1]
    edges = src_ref.shape[0]
    slots = edges // capacity
    pairs = slots // 2
    loads = [
        pltpu.make_async_copy(source, target, load_sems.at[index])
        for index, (source, target) in enumerate(
            (
                (inputs_hbm, inputs_ref),
                (embed_in_hbm, embed_in_ref),
                (embed_out_hbm, embed_out_ref),
                (values_hbm, values_ref),
            )
        )
    ]
    for load in loads[:3]:
        load.start()

    me = lax.axis_index("space")

    def clear(bin_, carry):
        filled[bin_] = 0
        for index in range(2):
            edge_of[bin_ * capacity + index] = 0
        return carry

    def clear_pair(pair, carry):
        crowded[pair] = 0
        return carry

    lax.fori_loop(0, slots * held, clear, 0)
    lax.fori_loop(0, pairs, clear_pair, 0)

    def sort(edge):
        bin_ = place_ref[dst_ref[edge]] ^ (me * held)
        count = filled[bin_]
        edge_of[bin_ * capacity + count] = edge
        filled[bin_] = count + 1
        pair = lax.div(bin_, 2 * held)
        seen = crowded[pair]
        crowded_of[pair * 2 * held + seen] = bin_
        crowded[pair] = seen + (count == 2).astype(jnp.int32)

    for load in loads[:3]:
        load.wait()
    loads[3].start()

    tiles = latent.shape[0] // tile_rows
    sorted_each = edges // tiles

    def embed(tile, carry):
        for index in range(sorted_each):
            sort(tile * sorted_each + index)
        first = pl.multiple_of(tile * tile_rows, tile_rows)
        columns = inputs_ref[:, pl.ds(first, tile_rows)]
        hidden = silu(transposed_matmul(columns, embed_in_ref[...])).astype(jnp.bfloat16)
        scaled = normalize(matmul(hidden, embed_out_ref[...])) * gain_ref[...]
        row = first + lax.broadcasted_iota(jnp.int32, (tile_rows, 1), 0)
        latent[pl.ds(first, tile_rows), :] = jnp.where(row < count_ref[0], scaled, 0.0).astype(jnp.bfloat16)
        return carry

    lax.fori_loop(0, tiles, embed, 0, unroll=True)
    for edge in range(tiles * sorted_each, edges):
        sort(edge)
    loads[3].wait()

    def stores(pair):
        copies = []
        for side in range(2):
            first = 0
            for chunk, order in enumerate(orders):
                count = held * cuts[chunk]
                start = pl.multiple_of(place_of(pair, order) * count, count)
                copies.append(
                    pltpu.make_async_copy(
                        staged.at[pair, side, pl.ds(first, count), :],
                        outs[side][chunk].at[pl.ds(start, count), :],
                        store_sems.at[pair, side, chunk],
                    )
                )
                first += count
        return copies

    def product(bin_, first, count):
        operator = []
        sources = []
        for index in range(first, first + 2):
            edge = jnp.where(count > index, edge_of[bin_ * capacity + index], 0)
            values = values_ref[edge]
            operator.append(jnp.where(count > index, values, jnp.zeros_like(values)))
            start = pl.multiple_of(src_ref[edge] * rows, rows)
            sources.append(latent[pl.ds(start, rows), :])
        return matmul(jnp.concatenate(operator, axis=1), jnp.concatenate(sources, axis=0))

    def stage(pair, side, block, summed):
        top = 0
        for cut in cuts:
            first = pl.multiple_of(top * held + block * cut, 16)
            staged[pair, side, pl.ds(first, cut), :] = summed[top : top + cut].astype(jnp.bfloat16)
            top += cut

    def multiply(turn, carry):
        for pair in (2 * turn, 2 * turn + 1):
            for side in range(2):
                for block in range(held):
                    bin_ = (2 * pair + side) * held + block
                    stage(pair, side, block, product(bin_, 0, filled[bin_]))

        def revisit(pair, index, carry):
            bin_ = crowded_of[pair * 2 * held + index]
            count = filled[bin_]
            summed = product(bin_, 0, count)
            for first in range(2, capacity, 2):
                summed = summed + product(bin_, first, count)
            stage(pair, lax.div(lax.rem(bin_, 2 * held), held), lax.rem(bin_, held), summed)
            return carry

        for pair in (2 * turn, 2 * turn + 1):
            lax.fori_loop(0, crowded[pair], functools.partial(revisit, pair), 0)
            for copy in stores(pair):
                copy.start()
        return carry

    lax.fori_loop(0, pairs // 2, multiply, 0)

    def finish(pair, carry):
        for copy in stores(pair):
            copy.wait()
        return carry

    lax.fori_loop(0, pairs, finish, 0)


def slab_sums(
    grid_inputs,
    grid_count,
    embed_in,
    embed_out,
    grid_gain,
    g2m_values,
    g2m_src,
    g2m_dst,
    mesh_place,
    partitions,
    orders,
    cuts,
):
    slab_rows = grid_inputs.shape[1]
    channels = embed_out.shape[1]
    edges, rows, _ = g2m_values.shape
    held = mesh_place.shape[0] // partitions
    capacity = edges // partitions
    pairs = partitions // 2
    shapes = [jax.ShapeDtypeStruct((pairs * held * cut, channels), jnp.bfloat16) for cut in cuts]
    return pl.pallas_call(
        functools.partial(grid_kernel, held, capacity, orders, cuts, min(512, slab_rows)),
        in_specs=[SMEM] * 4 + [VMEM] + [ANY] * 4,
        out_specs=[ANY] * (2 * len(cuts)),
        out_shape=shapes * 2,
        scratch_shapes=[
            pltpu.VMEM(grid_inputs.shape, jnp.bfloat16),
            pltpu.VMEM(embed_in.shape, jnp.bfloat16),
            pltpu.VMEM(embed_out.shape, jnp.bfloat16),
            pltpu.VMEM(g2m_values.shape, jnp.bfloat16),
            pltpu.VMEM((slab_rows, channels), jnp.bfloat16),
            pltpu.VMEM((pairs, 2, held * rows, channels), jnp.bfloat16),
            pltpu.SMEM((partitions * held * capacity,), jnp.int32),
            pltpu.SMEM((partitions * held,), jnp.int32),
            pltpu.SMEM((partitions * held + 1,), jnp.int32),
            pltpu.SMEM((pairs,), jnp.int32),
            pltpu.SemaphoreType.DMA((4,)),
            pltpu.SemaphoreType.DMA((pairs, 2, len(cuts))),
        ],
        compiler_params=pltpu.CompilerParams(vmem_limit_bytes=GRID_VMEM_BYTES),
        name="grid_to_mesh",
    )(
        g2m_src,
        g2m_dst,
        mesh_place,
        grid_count,
        grid_gain.reshape(1, -1),
        grid_inputs,
        embed_in,
        embed_out,
        g2m_values,
    )


def exchange(cells, bit):
    count = lax.axis_size("space")
    return lax.ppermute(cells, "space", [(i, i ^ (1 << bit)) for i in range(count)])


def reduce_chunks(mates, owns, orders, turns, later):
    arrived = [exchange(mate, 0) for mate in mates]
    kept = list(owns)
    made = [0] * len(orders)
    for turn, chunk in enumerate(turns):
        received = arrived[chunk]
        if turn > 0:
            received, _ = lax.optimization_barrier((received, previous))
        half = kept[chunk].shape[0] // 2
        previous = add(received[half:], kept[chunk][half:]).astype(jnp.bfloat16)
        kept[chunk] = add(received[:half], kept[chunk][:half]).astype(jnp.bfloat16)
        arrived[chunk] = exchange(previous, orders[chunk][made[chunk]])
        made[chunk] += 1
        if turn == len(orders) - 1:
            later = lax.optimization_barrier((later, previous))[0]
    return arrived, kept, later


def node_kernel(parts, reads, rows, mate_list_ref, other_list_ref, *refs):
    summands = refs[:parts]
    node_in_ref, node_out_ref, gain_ref, encoded_ref, own_ref, to_mate_ref, to_other_ref = refs[parts:]
    if parts == 1:
        summed = summands[0][...]
    else:
        chunks = parts // 2
        held = encoded_ref.shape[0] // rows
        pieces = [add(summands[chunk][...], summands[chunks + chunk][...]) for chunk in range(chunks)]
        cuts = [piece.shape[0] // held for piece in pieces]
        summed = jnp.concatenate(
            [
                piece[block * cut : (block + 1) * cut]
                for block in range(held)
                for piece, cut in zip(pieces, cuts)
            ],
            axis=0,
        )
    hidden = silu(matmul(summed.astype(jnp.bfloat16), node_in_ref[...])).astype(jnp.bfloat16)
    encoded = (summed + gain_ref[...] * normalize(matmul(hidden, node_out_ref[...]))).astype(jnp.bfloat16)
    encoded_ref[...] = encoded
    own_ref[...] = encoded
    odd = lax.rem(lax.axis_index("space"), 2)
    for index in range(reads):
        for wanted_ref, first, out in (
            (mate_list_ref, odd * reads, to_mate_ref),
            (other_list_ref, (1 - odd) * reads, to_other_ref),
        ):
            start = pl.multiple_of(wanted_ref[0, first + index] * rows, rows)
            out[index * rows : (index + 1) * rows, :] = encoded_ref[pl.ds(start, rows), :]


def encode(summands, node_in, node_out, node_gain, lists, held, rows):
    channels = node_in.shape[0]
    reads = lists[0].shape[1] // 2
    return pl.pallas_call(
        functools.partial(node_kernel, len(summands), reads, rows),
        in_specs=[SMEM] * 2 + [VMEM] * (len(summands) + 3),
        out_specs=[VMEM] * 4,
        out_shape=[
            jax.ShapeDtypeStruct((held * rows, channels), jnp.bfloat16),
            jax.ShapeDtypeStruct((held * rows, channels), jnp.bfloat16),
            jax.ShapeDtypeStruct((reads * rows, channels), jnp.bfloat16),
            jax.ShapeDtypeStruct((reads * rows, channels), jnp.bfloat16),
        ],
        compiler_params=pltpu.CompilerParams(vmem_limit_bytes=VMEM_BYTES),
        name="node_update",
    )(*lists, *summands, node_in, node_out, node_gain.reshape(1, -1))


def operator_kernel(held, reads, dst_ref, src_ref, values_ref, operator_ref, total):
    edges, rows, _ = values_ref.shape
    odd = lax.rem(lax.axis_index("space"), 2)
    total[...] = jnp.zeros_like(total)
    for edge in range(edges):
        side = lax.div(src_ref[edge], held)
        index = lax.rem(src_ref[edge], held)
        across = (odd + lax.div(side, 2) + 1) & 1
        source = jnp.where(side == 1, 2 * reads, across * reads) + index
        first = pl.multiple_of(dst_ref[edge] * rows, rows)
        total[source, pl.ds(first, rows), :] += values_ref[edge].astype(jnp.float32)
    for source in range(2 * reads + held):
        operator_ref[:, source * rows : (source + 1) * rows] = total[source].astype(jnp.bfloat16)


def mesh_operator(mesh_values, mesh_dst, mesh_src, held, reads):
    rows = mesh_values.shape[1]
    sources = 2 * reads + held
    return pl.pallas_call(
        functools.partial(operator_kernel, held, reads),
        in_specs=[SMEM] * 2 + [VMEM],
        out_specs=VMEM,
        out_shape=jax.ShapeDtypeStruct((held * rows, sources * rows), jnp.bfloat16),
        scratch_shapes=[pltpu.VMEM((sources, held * rows, rows), jnp.float32)],
        compiler_params=pltpu.CompilerParams(vmem_limit_bytes=VMEM_BYTES),
        name="mesh_operator",
    )(mesh_dst, mesh_src, mesh_values)


def process_kernel(
    operator_ref, own_ref, mate_ref, other_ref, proc_in_ref, proc_out_ref, gain_ref, processed_ref
):
    message = 0.0
    first = 0
    for source_ref in (mate_ref, other_ref, own_ref):
        last = first + source_ref.shape[0]
        message = message + matmul(operator_ref[:, first:last], source_ref[...])
        first = last
    hidden = silu(matmul(message.astype(jnp.bfloat16), proc_in_ref[...])).astype(jnp.bfloat16)
    update = gain_ref[...] * normalize(matmul(hidden, proc_out_ref[...]))
    processed_ref[...] = (own_ref[...].astype(jnp.float32) + update).astype(jnp.bfloat16)


def process(operator, own, from_mate, from_other, proc_in, proc_out, proc_gain):
    return pl.pallas_call(
        process_kernel,
        in_specs=[VMEM] * 7,
        out_specs=VMEM,
        out_shape=jax.ShapeDtypeStruct(own.shape, jnp.bfloat16),
        compiler_params=pltpu.CompilerParams(vmem_limit_bytes=VMEM_BYTES),
        name="process",
    )(operator, own, from_mate, from_other, proc_in, proc_out, proc_gain.reshape(1, -1))


def lookup(table, wanted):
    matches = wanted[:, None] == jnp.arange(table.shape[0], dtype=jnp.int32)[None, :]
    return jnp.sum(jnp.where(matches, table[None, :], 0), axis=1)


def routed_sum(
    grid_inputs, grid_count, embed_in, embed_out, grid_gain, g2m_values, g2m_src, g2m_dst, mesh_place, partitions
):
    slab_rows = grid_inputs.shape[1]
    edge_count, block_rows, _ = g2m_values.shape
    channels = embed_out.shape[1]
    held = mesh_place.shape[0] // partitions
    capacity = max(1, (edge_count + partitions - 1) // partitions)
    slot_count = partitions * capacity
    hidden = jax.nn.silu(transposed_matmul(grid_inputs, embed_in)).astype(jnp.bfloat16)
    alive = lax.iota(jnp.int32, slab_rows) < grid_count[0]
    latent = jnp.where(alive[:, None], normalize(matmul(hidden, embed_out)) * grid_gain, 0.0).astype(jnp.bfloat16)
    positions = lookup(mesh_place, g2m_dst)
    targets = positions // held
    ranking = jnp.sum(jnp.tril(targets[:, None] == targets[None, :], -1), axis=1)
    slot_index = targets * capacity + ranking
    labels = jnp.full((slot_count,), -1, jnp.int32).at[slot_index].set(positions % held)
    sources = latent.reshape(slab_rows // block_rows, block_rows, channels)[g2m_src]
    terms = jnp.einsum("eij,ejd->eid", g2m_values, sources, preferred_element_type=jnp.float32).astype(jnp.bfloat16)
    outgoing = jnp.zeros((slot_count, block_rows, channels), jnp.bfloat16).at[slot_index].set(terms)
    arrived = lax.all_to_all(outgoing, "space", split_axis=0, concat_axis=0, tiled=True)
    arrived_labels = lax.all_to_all(labels, "space", split_axis=0, concat_axis=0, tiled=True)
    selector = (arrived_labels[None, :] == jnp.arange(held, dtype=jnp.int32)[:, None]).astype(jnp.bfloat16)
    return matmul(selector, arrived.reshape(slot_count, -1)).reshape(held * block_rows, channels)


def shards(
    grid_inputs,
    grid_count,
    embed_in,
    embed_out,
    grid_gain,
    g2m_values,
    g2m_src,
    g2m_dst,
    mesh_place,
    node_in,
    node_out,
    node_gain,
    recv_blocks,
    mesh_values,
    mesh_dst,
    mesh_src,
    proc_in,
    proc_out,
    proc_gain,
):
    partitions = lax.axis_size("space")
    edges, rows, _ = g2m_values.shape
    mesh_blocks = mesh_place.shape[0]
    held = mesh_blocks // partitions
    reads = recv_blocks.shape[1] // 2
    mates = [(i, i ^ 1) for i in range(partitions)]
    others = [(i, (i + 1 if i % 2 else i - 1) % partitions) for i in range(partitions)]
    grid_args = (grid_inputs, grid_count, embed_in, embed_out, grid_gain, g2m_values, g2m_src, g2m_dst, mesh_place)
    if partitions == 1 << (1 + len(ORDERS[0])) and edges % partitions == 0 and edges >= mesh_blocks:
        cuts = [share * rows // sum(SHARES) for share in SHARES]
        sums = slab_sums(*grid_args, partitions, ORDERS, cuts)
        arrived, kept, (recv_blocks, mesh_values) = reduce_chunks(
            sums[: len(cuts)], sums[len(cuts) :], ORDERS, TURNS, (recv_blocks, mesh_values)
        )
        summands = arrived + kept
    else:
        summands = [routed_sum(*grid_args, partitions)]
    lists = (lax.ppermute(recv_blocks, "space", mates), lax.ppermute(recv_blocks, "space", others))
    operator = mesh_operator(mesh_values, mesh_dst, mesh_src, held, reads)
    encoded, own, to_mate, to_other = encode(summands, node_in, node_out, node_gain, lists, held, rows)
    from_other = lax.ppermute(to_other, "space", others)
    from_mate = lax.ppermute(to_mate, "space", mates)
    processed = process(operator, own, from_mate, from_other, proc_in, proc_out, proc_gain)
    return (encoded, processed)


def solution(mesh):
    return jax.shard_map(
        shards,
        mesh=mesh,
        in_specs=(
            P(None, ("groups", "space")),
            P("space"),
            P(),
            P(),
            P(),
            P("space", None, None),
            P("space"),
            P("space"),
            P(),
            P(),
            P(),
            P(),
            P("space", None),
            P("space", None, None),
            P("space"),
            P("space"),
            P(),
            P(),
            P(),
        ),
        out_specs=(P(("groups", "space"), None), P(("groups", "space"), None)),
        check_vma=False,
    )
```

```python
import functools

import jax
import jax.numpy as jnp
from jax import lax
from jax.experimental import pallas as pl
from jax.experimental.pallas import tpu as pltpu
from jax.sharding import PartitionSpec as P

EPSILON = 1e-05
ORDERS = ((1, 2, 3), (2, 1, 3), (3, 1, 2), (1, 2, 3))
SHARES = (2, 2, 2, 2)
TURNS = (2, 0, 1, 3, 0, 1, 2, 3, 0, 1, 2, 3)
EARLY = 1
VMEM_BYTES = 24 * 1024 * 1024
GRID_VMEM_BYTES = 60 * 1024 * 1024
VMEM = pl.BlockSpec(memory_space=pltpu.VMEM)
SMEM = pl.BlockSpec(memory_space=pltpu.SMEM)
ANY = pl.BlockSpec(memory_space=pl.ANY)


def silu(values):
    half = 0.5 * values
    return half + half * jnp.tanh(half)


def normalize(values):
    average = jnp.mean(values, axis=-1, keepdims=True)
    centred = values - average
    variance = jnp.mean(centred * centred, axis=-1, keepdims=True)
    return centred * lax.rsqrt(variance + EPSILON)


def matmul(left, right):
    return jnp.dot(left, right, preferred_element_type=jnp.float32)


def transposed_matmul(left, right):
    return lax.dot_general(left, right, (((0,), (0,)), ((), ())), preferred_element_type=jnp.float32)


def add(left, right):
    return left.astype(jnp.float32) + right.astype(jnp.float32)


def place_of(step, order):
    place = 0
    for bit in order:
        place = place * 2 + ((step >> (bit - 1)) & 1)
    return place


def grid_kernel(
    held,
    capacity,
    orders,
    cuts,
    tile_rows,
    src_ref,
    dst_ref,
    place_ref,
    count_ref,
    gain_ref,
    inputs_hbm,
    embed_in_hbm,
    embed_out_hbm,
    values_hbm,
    *refs,
):
    chunks = len(orders)
    outs = (refs[chunks : 2 * chunks], refs[:chunks])
    (
        inputs_ref,
        embed_in_ref,
        embed_out_ref,
        values_ref,
        latent,
        staged,
        edge_of,
        filled,
        crowded_of,
        crowded,
        load_sems,
        store_sems,
    ) = refs[2 * chunks :]
    rows = values_ref.shape[1]
    edges = src_ref.shape[0]
    slots = edges // capacity
    pairs = slots // 2
    loads = [
        pltpu.make_async_copy(source, target, load_sems.at[index])
        for index, (source, target) in enumerate(
            (
                (inputs_hbm, inputs_ref),
                (embed_in_hbm, embed_in_ref),
                (embed_out_hbm, embed_out_ref),
                (values_hbm, values_ref),
            )
        )
    ]
    for load in loads[:3]:
        load.start()

    me = lax.axis_index("space")

    def clear(bin_, carry):
        filled[bin_] = 0
        for index in range(2):
            edge_of[bin_ * capacity + index] = 0
        return carry

    def clear_pair(pair, carry):
        crowded[pair] = 0
        return carry

    lax.fori_loop(0, slots * held, clear, 0)
    lax.fori_loop(0, pairs, clear_pair, 0)

    def sort(edge):
        bin_ = place_ref[dst_ref[edge]] ^ (me * held)
        count = filled[bin_]
        edge_of[bin_ * capacity + count] = edge
        filled[bin_] = count + 1
        pair = lax.div(bin_, 2 * held)
        seen = crowded[pair]
        crowded_of[pair * 2 * held + seen] = bin_
        crowded[pair] = seen + (count == 2).astype(jnp.int32)

    for load in loads[:3]:
        load.wait()
    loads[3].start()

    tiles = latent.shape[0] // tile_rows
    sorted_each = edges // tiles

    def embed(tile, carry):
        for index in range(sorted_each):
            sort(tile * sorted_each + index)
        first = pl.multiple_of(tile * tile_rows, tile_rows)
        columns = inputs_ref[:, pl.ds(first, tile_rows)]
        hidden = silu(transposed_matmul(columns, embed_in_ref[...])).astype(jnp.bfloat16)
        scaled = normalize(matmul(hidden, embed_out_ref[...])) * gain_ref[...]
        row = first + lax.broadcasted_iota(jnp.int32, (tile_rows, 1), 0)
        latent[pl.ds(first, tile_rows), :] = jnp.where(row < count_ref[0], scaled, 0.0).astype(jnp.bfloat16)
        return carry

    lax.fori_loop(0, tiles, embed, 0, unroll=True)
    for edge in range(tiles * sorted_each, edges):
        sort(edge)
    loads[3].wait()

    def stores(pair):
        copies = []
        for side in range(2):
            first = 0
            for chunk, order in enumerate(orders):
                count = held * cuts[chunk]
                start = pl.multiple_of(place_of(pair, order) * count, count)
                copies.append(
                    pltpu.make_async_copy(
                        staged.at[pair, side, pl.ds(first, count), :],
                        outs[side][chunk].at[pl.ds(start, count), :],
                        store_sems.at[pair, side, chunk],
                    )
                )
                first += count
        return copies

    def product(bin_, first, count):
        operator = []
        sources = []
        for index in range(first, first + 2):
            edge = jnp.where(count > index, edge_of[bin_ * capacity + index], 0)
            values = values_ref[edge]
            operator.append(jnp.where(count > index, values, jnp.zeros_like(values)))
            start = pl.multiple_of(src_ref[edge] * rows, rows)
            sources.append(latent[pl.ds(start, rows), :])
        return matmul(jnp.concatenate(operator, axis=1), jnp.concatenate(sources, axis=0))

    def stage(pair, side, block, summed):
        top = 0
        for cut in cuts:
            first = pl.multiple_of(top * held + block * cut, 16)
            staged[pair, side, pl.ds(first, cut), :] = summed[top : top + cut].astype(jnp.bfloat16)
            top += cut

    def multiply(turn, carry):
        for pair in (2 * turn, 2 * turn + 1):
            for side in range(2):
                for block in range(held):
                    bin_ = (2 * pair + side) * held + block
                    stage(pair, side, block, product(bin_, 0, filled[bin_]))

        def revisit(pair, index, carry):
            bin_ = crowded_of[pair * 2 * held + index]
            count = filled[bin_]
            summed = product(bin_, 0, count)
            for first in range(2, capacity, 2):
                summed = summed + product(bin_, first, count)
            stage(pair, lax.div(lax.rem(bin_, 2 * held), held), lax.rem(bin_, held), summed)
            return carry

        for pair in (2 * turn, 2 * turn + 1):
            lax.fori_loop(0, crowded[pair], functools.partial(revisit, pair), 0)
            for copy in stores(pair):
                copy.start()
        return carry

    lax.fori_loop(0, pairs // 2, multiply, 0)

    def finish(pair, carry):
        for copy in stores(pair):
            copy.wait()
        return carry

    lax.fori_loop(0, pairs, finish, 0)


def slab_sums(
    grid_inputs,
    grid_count,
    embed_in,
    embed_out,
    grid_gain,
    g2m_values,
    g2m_src,
    g2m_dst,
    mesh_place,
    partitions,
    orders,
    cuts,
):
    slab_rows = grid_inputs.shape[1]
    channels = embed_out.shape[1]
    edges, rows, _ = g2m_values.shape
    held = mesh_place.shape[0] // partitions
    capacity = edges // partitions
    pairs = partitions // 2
    shapes = [jax.ShapeDtypeStruct((pairs * held * cut, channels), jnp.bfloat16) for cut in cuts]
    return pl.pallas_call(
        functools.partial(grid_kernel, held, capacity, orders, cuts, min(512, slab_rows)),
        in_specs=[SMEM] * 4 + [VMEM] + [ANY] * 4,
        out_specs=[ANY] * (2 * len(cuts)),
        out_shape=shapes * 2,
        scratch_shapes=[
            pltpu.VMEM(grid_inputs.shape, jnp.bfloat16),
            pltpu.VMEM(embed_in.shape, jnp.bfloat16),
            pltpu.VMEM(embed_out.shape, jnp.bfloat16),
            pltpu.VMEM(g2m_values.shape, jnp.bfloat16),
            pltpu.VMEM((slab_rows, channels), jnp.bfloat16),
            pltpu.VMEM((pairs, 2, held * rows, channels), jnp.bfloat16),
            pltpu.SMEM((partitions * held * capacity,), jnp.int32),
            pltpu.SMEM((partitions * held,), jnp.int32),
            pltpu.SMEM((partitions * held + 1,), jnp.int32),
            pltpu.SMEM((pairs,), jnp.int32),
            pltpu.SemaphoreType.DMA((4,)),
            pltpu.SemaphoreType.DMA((pairs, 2, len(cuts))),
        ],
        compiler_params=pltpu.CompilerParams(vmem_limit_bytes=GRID_VMEM_BYTES),
        name="grid_to_mesh",
    )(
        g2m_src,
        g2m_dst,
        mesh_place,
        grid_count,
        grid_gain.reshape(1, -1),
        grid_inputs,
        embed_in,
        embed_out,
        g2m_values,
    )


def exchange(cells, bit):
    count = lax.axis_size("space")
    return lax.ppermute(cells, "space", [(i, i ^ (1 << bit)) for i in range(count)])


def reduce_chunks(mates, owns, orders, turns, lists):
    arrived = [exchange(mate, 0) for mate in mates]
    kept = list(owns)
    made = [0] * len(orders)
    for turn, chunk in enumerate(turns):
        received = arrived[chunk]
        if turn == len(orders):
            received, _, lists = lax.optimization_barrier((received, previous, lists))
        elif turn > 0:
            received, _ = lax.optimization_barrier((received, previous))
        half = kept[chunk].shape[0] // 2
        previous = add(received[half:], kept[chunk][half:]).astype(jnp.bfloat16)
        kept[chunk] = add(received[:half], kept[chunk][:half]).astype(jnp.bfloat16)
        arrived[chunk] = exchange(previous, orders[chunk][made[chunk]])
        made[chunk] += 1
    return arrived, kept, lists


def node_kernel(held, parts, earlier, reads, mate_list_ref, other_list_ref, *refs):
    summands, refs = refs[:parts], refs[parts:]
    if earlier:
        earlier_ref, refs = refs[0], refs[1:]
    node_in_ref, node_out_ref, gain_ref, to_mate_ref, to_other_ref = refs[:5]
    encoded_refs = refs[5:]
    if parts == 1:
        summed = summands[0][...]
    else:
        pieces = []
        for block in range(held):
            for arrived, kept in zip(summands[: parts // 2], summands[parts // 2 :]):
                cut = arrived.shape[0] // held
                piece = slice(block * cut, (block + 1) * cut)
                pieces.append(add(arrived[piece, :], kept[piece, :]))
        summed = jnp.concatenate(pieces, axis=0)
    rows = summed.shape[0] // held
    hidden = silu(matmul(summed.astype(jnp.bfloat16), node_in_ref[...])).astype(jnp.bfloat16)
    encoded = (summed + gain_ref[...] * normalize(matmul(hidden, node_out_ref[...]))).astype(jnp.bfloat16)
    for out in encoded_refs:
        if earlier:
            ahead = earlier_ref.shape[0] // held
            for block in range(held):
                first = block * (ahead + rows)
                out[first : first + ahead, :] = earlier_ref[block * ahead : (block + 1) * ahead, :]
                out[first + ahead : first + ahead + rows, :] = encoded[block * rows : (block + 1) * rows]
        else:
            out[...] = encoded
    encoded_ref = encoded_refs[0]
    odd = lax.rem(lax.axis_index("space"), 2)
    whole = encoded_ref.shape[0] // held
    for index in range(reads):
        for wanted_ref, first, out in (
            (mate_list_ref, odd * reads, to_mate_ref),
            (other_list_ref, (1 - odd) * reads, to_other_ref),
        ):
            start = pl.multiple_of(wanted_ref[0, first + index] * whole + (whole - rows), 16)
            out[index * rows : (index + 1) * rows, :] = encoded_ref[pl.ds(start, rows), :]


def encode(summands, earlier, node_in, node_out, node_gain, lists, held, copies):
    channels = node_in.shape[0]
    reads = lists[0].shape[1] // 2
    count = sum(summand.shape[0] for summand in summands) // (2 if len(summands) > 1 else 1)
    sent = jax.ShapeDtypeStruct((count // held * reads, channels), jnp.bfloat16)
    total = jax.ShapeDtypeStruct((count + sum(part.shape[0] for part in earlier), channels), jnp.bfloat16)
    return pl.pallas_call(
        functools.partial(node_kernel, held, len(summands), len(earlier), reads),
        in_specs=[SMEM] * 2 + [VMEM] * (len(summands) + len(earlier) + 3),
        out_specs=[VMEM] * (2 + copies),
        out_shape=[sent] * 2 + [total] * copies,
        compiler_params=pltpu.CompilerParams(vmem_limit_bytes=VMEM_BYTES),
        name="node_update",
    )(*lists, *summands, *earlier, node_in, node_out, node_gain.reshape(1, -1))


def operator_kernel(held, reads, splits, dst_ref, src_ref, values_ref, operator_ref, total):
    edges, rows, _ = values_ref.shape
    odd = lax.rem(lax.axis_index("space"), 2)
    total[...] = jnp.zeros_like(total)
    for edge in range(edges):
        side = lax.div(src_ref[edge], held)
        index = lax.rem(src_ref[edge], held)
        across = (odd + lax.div(side, 2) + 1) & 1
        source = jnp.where(side == 1, 2 * reads, across * reads) + index
        first = pl.multiple_of(dst_ref[edge] * rows, rows)
        total[source, pl.ds(first, rows), :] += values_ref[edge].astype(jnp.float32)
    columns = [
        total[source][:, low:high].astype(jnp.bfloat16) for low, high in splits for source in range(2 * reads)
    ]
    columns += [total[source].astype(jnp.bfloat16) for source in range(2 * reads, 2 * reads + held)]
    operator_ref[...] = jnp.concatenate(columns, axis=1)


def mesh_operator(mesh_values, mesh_dst, mesh_src, held, reads, splits):
    rows = mesh_values.shape[1]
    sources = 2 * reads + held
    return pl.pallas_call(
        functools.partial(operator_kernel, held, reads, splits),
        in_specs=[SMEM] * 2 + [VMEM],
        out_specs=VMEM,
        out_shape=jax.ShapeDtypeStruct((held * rows, sources * rows), jnp.bfloat16),
        scratch_shapes=[pltpu.VMEM((sources, held * rows, rows), jnp.float32)],
        compiler_params=pltpu.CompilerParams(vmem_limit_bytes=VMEM_BYTES),
        name="mesh_operator",
    )(mesh_dst, mesh_src, mesh_values)


def process_kernel(operator_ref, own_ref, *refs):
    halos, (proc_in_ref, proc_out_ref, gain_ref, processed_ref) = refs[:-4], refs[-4:]
    sources = jnp.concatenate([halo[...] for halo in halos] + [own_ref[...]], axis=0)
    message = matmul(operator_ref[...], sources)
    hidden = silu(matmul(message.astype(jnp.bfloat16), proc_in_ref[...])).astype(jnp.bfloat16)
    update = gain_ref[...] * normalize(matmul(hidden, proc_out_ref[...]))
    processed_ref[...] = (own_ref[...].astype(jnp.float32) + update).astype(jnp.bfloat16)


def process(operator, own, halos, proc_in, proc_out, proc_gain):
    return pl.pallas_call(
        process_kernel,
        in_specs=[VMEM] * (5 + len(halos)),
        out_specs=VMEM,
        out_shape=jax.ShapeDtypeStruct(own.shape, jnp.bfloat16),
        compiler_params=pltpu.CompilerParams(vmem_limit_bytes=VMEM_BYTES),
        name="process",
    )(operator, own, *halos, proc_in, proc_out, proc_gain.reshape(1, -1))


def lookup(table, wanted):
    matches = wanted[:, None] == jnp.arange(table.shape[0], dtype=jnp.int32)[None, :]
    return jnp.sum(jnp.where(matches, table[None, :], 0), axis=1)


def routed_sum(
    grid_inputs, grid_count, embed_in, embed_out, grid_gain, g2m_values, g2m_src, g2m_dst, mesh_place, partitions
):
    slab_rows = grid_inputs.shape[1]
    edge_count, block_rows, _ = g2m_values.shape
    channels = embed_out.shape[1]
    held = mesh_place.shape[0] // partitions
    capacity = max(1, (edge_count + partitions - 1) // partitions)
    slot_count = partitions * capacity
    hidden = jax.nn.silu(transposed_matmul(grid_inputs, embed_in)).astype(jnp.bfloat16)
    alive = lax.iota(jnp.int32, slab_rows) < grid_count[0]
    latent = jnp.where(alive[:, None], normalize(matmul(hidden, embed_out)) * grid_gain, 0.0).astype(jnp.bfloat16)
    positions = lookup(mesh_place, g2m_dst)
    targets = positions // held
    ranking = jnp.sum(jnp.tril(targets[:, None] == targets[None, :], -1), axis=1)
    slot_index = targets * capacity + ranking
    labels = jnp.full((slot_count,), -1, jnp.int32).at[slot_index].set(positions % held)
    sources = latent.reshape(slab_rows // block_rows, block_rows, channels)[g2m_src]
    terms = jnp.einsum("eij,ejd->eid", g2m_values, sources, preferred_element_type=jnp.float32).astype(jnp.bfloat16)
    outgoing = jnp.zeros((slot_count, block_rows, channels), jnp.bfloat16).at[slot_index].set(terms)
    arrived = lax.all_to_all(outgoing, "space", split_axis=0, concat_axis=0, tiled=True)
    arrived_labels = lax.all_to_all(labels, "space", split_axis=0, concat_axis=0, tiled=True)
    selector = (arrived_labels[None, :] == jnp.arange(held, dtype=jnp.int32)[:, None]).astype(jnp.bfloat16)
    return matmul(selector, arrived.reshape(slot_count, -1)).reshape(held * block_rows, channels)


def shards(
    grid_inputs,
    grid_count,
    embed_in,
    embed_out,
    grid_gain,
    g2m_values,
    g2m_src,
    g2m_dst,
    mesh_place,
    node_in,
    node_out,
    node_gain,
    recv_blocks,
    mesh_values,
    mesh_dst,
    mesh_src,
    proc_in,
    proc_out,
    proc_gain,
):
    partitions = lax.axis_size("space")
    edges, rows, _ = g2m_values.shape
    mesh_blocks = mesh_place.shape[0]
    held = mesh_blocks // partitions
    reads = recv_blocks.shape[1] // 2
    mates = [(i, i ^ 1) for i in range(partitions)]
    others = [(i, (i + 1 if i % 2 else i - 1) % partitions) for i in range(partitions)]
    grid_args = (grid_inputs, grid_count, embed_in, embed_out, grid_gain, g2m_values, g2m_src, g2m_dst, mesh_place)
    lists = (lax.ppermute(recv_blocks, "space", mates), lax.ppermute(recv_blocks, "space", others))
    splits = [(0, rows)]
    halos = []
    earlier = []
    if partitions == 1 << (1 + len(ORDERS[0])) and edges % partitions == 0 and edges >= mesh_blocks:
        cuts = [share * rows // sum(SHARES) for share in SHARES]
        sums = slab_sums(*grid_args, partitions, ORDERS, cuts)
        arrived, kept, lists = reduce_chunks(sums[: len(cuts)], sums[len(cuts) :], ORDERS, TURNS, lists)
        if EARLY:
            first = sum(cuts[:EARLY])
            splits = [(0, first), (first, rows)]
            to_mate, to_other, ahead = encode(
                arrived[:EARLY] + kept[:EARLY], [], node_in, node_out, node_gain, lists, held, 1
            )
            halos = [lax.ppermute(to_mate, "space", mates), lax.ppermute(to_other, "space", others)]
            arrived[-1], ahead, halos = lax.optimization_barrier((arrived[-1], ahead, halos))
            earlier = [ahead]
        summands = arrived[EARLY:] + kept[EARLY:]
    else:
        summands = [routed_sum(*grid_args, partitions)]
    operator = mesh_operator(mesh_values, mesh_dst, mesh_src, held, reads, splits)
    to_mate, to_other, encoded, own = encode(summands, earlier, node_in, node_out, node_gain, lists, held, 2)
    halos += [lax.ppermute(to_mate, "space", mates), lax.ppermute(to_other, "space", others)]
    processed = process(operator, own, halos, proc_in, proc_out, proc_gain)
    return (encoded, processed)


def solution(mesh):
    return jax.shard_map(
        shards,
        mesh=mesh,
        in_specs=(
            P(None, ("groups", "space")),
            P("space"),
            P(),
            P(),
            P(),
            P("space", None, None),
            P("space"),
            P("space"),
            P(),
            P(),
            P(),
            P(),
            P("space", None),
            P("space", None, None),
            P("space"),
            P("space"),
            P(),
            P(),
            P(),
        ),
        out_specs=(P(("groups", "space"), None), P(("groups", "space"), None)),
        check_vma=False,
    )
```

```python
import functools

import jax
import jax.numpy as jnp
from jax import lax
from jax.experimental import pallas as pl
from jax.experimental.pallas import tpu as pltpu
from jax.sharding import PartitionSpec as P

EPSILON = 1e-05
ORDERS = ((1, 2, 3), (2, 1, 3), (3, 1, 2), (1, 2, 3))
SHARES = (2, 2, 2, 2)
TURNS = (2, 0, 1, 3, 0, 1, 2, 3, 0, 1, 2, 3)
EARLY = 1
VMEM_BYTES = 24 * 1024 * 1024
GRID_VMEM_BYTES = 43 * 1024 * 1024
VMEM = pl.BlockSpec(memory_space=pltpu.VMEM)
SMEM = pl.BlockSpec(memory_space=pltpu.SMEM)
HBM = pl.BlockSpec(memory_space=pltpu.HBM)


def silu(values):
    half = 0.5 * values
    return half + half * jnp.tanh(half)


def normalize(values):
    average = jnp.mean(values, axis=-1, keepdims=True)
    centred = values - average
    variance = jnp.mean(centred * centred, axis=-1, keepdims=True)
    return centred * lax.rsqrt(variance + EPSILON)


def matmul(left, right):
    return jnp.dot(left, right, preferred_element_type=jnp.float32)


def transposed_matmul(left, right):
    return lax.dot_general(left, right, (((0,), (0,)), ((), ())), preferred_element_type=jnp.float32)


def add(left, right):
    return left.astype(jnp.float32) + right.astype(jnp.float32)


def place_of(step, order):
    place = 0
    for bit in order:
        place = place * 2 + ((step >> (bit - 1)) & 1)
    return place


def grid_kernel(
    held,
    capacity,
    orders,
    cuts,
    tile_rows,
    edges,
    table_ref,
    inputs_ref,
    embed_in_ref,
    embed_out_ref,
    values_hbm,
    *refs,
):
    chunks = len(orders)
    outs = (refs[chunks : 2 * chunks], refs[:chunks])
    (
        values_ref,
        latent,
        edge_of,
        filled,
        crowded_of,
        crowded,
        load_sem,
    ) = refs[2 * chunks :]
    rows = values_ref.shape[1]
    slots = edges // capacity
    pairs = slots // 2
    load = pltpu.make_async_copy(values_hbm, values_ref, load_sem)
    load.start()

    me = lax.axis_index("space")

    def clear(bin_, carry):
        filled[bin_] = 0
        for index in range(2):
            edge_of[bin_ * capacity + index] = 0
        return carry

    lax.fori_loop(0, slots * held, clear, 0)
    crowded[0] = 0

    def sort(edge):
        bin_ = table_ref[2 * edges + table_ref[edges + edge]] ^ (me * held)
        count = filled[bin_]
        edge_of[bin_ * capacity + count] = edge
        filled[bin_] = count + 1
        seen = crowded[0]
        crowded_of[seen] = bin_
        crowded[0] = seen + (count == 2).astype(jnp.int32)


    alive = table_ref[table_ref.shape[0] - 1]
    tiles = latent.shape[0] // tile_rows
    sorted_each = edges // tiles

    def embed(tile, carry):
        for index in range(sorted_each):
            sort(tile * sorted_each + index)
        first = pl.multiple_of(tile * tile_rows, tile_rows)
        columns = inputs_ref[:, pl.ds(first, tile_rows)]
        hidden = silu(transposed_matmul(columns, embed_in_ref[...])).astype(jnp.bfloat16)
        normal = normalize(matmul(hidden, embed_out_ref[...]))
        row = first + lax.broadcasted_iota(jnp.int32, (tile_rows, 1), 0)
        latent[pl.ds(first, tile_rows), :] = jnp.where(row < alive, normal, 0.0).astype(jnp.bfloat16)
        return carry

    lax.fori_loop(0, tiles, embed, 0, unroll=True)
    for edge in range(tiles * sorted_each, edges):
        sort(edge)
    load.wait()

    def product(bin_, first, count):
        operator = []
        sources = []
        for index in range(first, first + 2):
            edge = jnp.where(count > index, edge_of[bin_ * capacity + index], 0)
            values = values_ref[edge]
            operator.append(jnp.where(count > index, values, jnp.zeros_like(values)))
            start = pl.multiple_of(table_ref[edge] * rows, rows)
            sources.append(latent[pl.ds(start, rows), :])
        return matmul(jnp.concatenate(operator, axis=1), jnp.concatenate(sources, axis=0))

    def store(pair, side, block, summed):
        top = 0
        for out, order, cut in zip(outs[side], orders, cuts):
            first = pl.multiple_of((place_of(pair, order) * held + block) * cut, 16)
            out[pl.ds(first, cut), :] = summed[top : top + cut].astype(jnp.bfloat16)
            top += cut

    def multiply(turn, carry):
        for pair in (2 * turn, 2 * turn + 1):
            for side in range(2):
                for block in range(held):
                    bin_ = (2 * pair + side) * held + block
                    store(pair, side, block, product(bin_, 0, filled[bin_]))

        return carry

    lax.fori_loop(0, pairs // 2, multiply, 0)

    def revisit(index, carry):
        bin_ = crowded_of[index]
        count = filled[bin_]
        summed = product(bin_, 0, count)
        for first in range(2, capacity, 2):
            summed = summed + product(bin_, first, count)
        pair = lax.div(bin_, 2 * held)
        side = lax.rem(lax.div(bin_, held), 2)
        for each in range(2):

            @pl.when(side == each)
            def _(each=each):
                store(pair, each, lax.rem(bin_, held), summed)

        return carry

    lax.fori_loop(0, crowded[0], revisit, 0)


def slab_sums(
    grid_inputs,
    grid_count,
    embed_in,
    embed_out,
    g2m_values,
    g2m_src,
    g2m_dst,
    mesh_place,
    partitions,
    orders,
    cuts,
):
    slab_rows = grid_inputs.shape[1]
    channels = embed_out.shape[1]
    edges, rows, _ = g2m_values.shape
    held = mesh_place.shape[0] // partitions
    capacity = edges // partitions
    pairs = partitions // 2
    shapes = [jax.ShapeDtypeStruct((pairs * held * cut, channels), jnp.bfloat16) for cut in cuts]
    return pl.pallas_call(
        functools.partial(grid_kernel, held, capacity, orders, cuts, min(512, slab_rows), edges),
        in_specs=[SMEM] + [VMEM] * 3 + [HBM],
        out_specs=[VMEM] * (2 * len(cuts)),
        out_shape=shapes * 2,
        scratch_shapes=[
            pltpu.VMEM(g2m_values.shape, jnp.bfloat16),
            pltpu.VMEM((slab_rows, channels), jnp.bfloat16),
            pltpu.SMEM((partitions * held * capacity,), jnp.int32),
            pltpu.SMEM((partitions * held,), jnp.int32),
            pltpu.SMEM((partitions * held + 1,), jnp.int32),
            pltpu.SMEM((1,), jnp.int32),
            pltpu.SemaphoreType.DMA,
        ],
        compiler_params=pltpu.CompilerParams(vmem_limit_bytes=GRID_VMEM_BYTES),
        name="grid_to_mesh",
    )(jnp.concatenate([g2m_src, g2m_dst, mesh_place, grid_count]), grid_inputs, embed_in, embed_out, g2m_values)


def exchange(cells, bit):
    count = lax.axis_size("space")
    return lax.ppermute(cells, "space", [(i, i ^ (1 << bit)) for i in range(count)])


def reduce_chunks(mates, owns, orders, turns, lists):
    arrived = [exchange(mate, 0) for mate in mates]
    kept = list(owns)
    made = [0] * len(orders)
    for turn, chunk in enumerate(turns):
        received = arrived[chunk]
        if turn == len(orders):
            received, _, lists = lax.optimization_barrier((received, previous, lists))
        elif turn > 0:
            received, _ = lax.optimization_barrier((received, previous))
        half = kept[chunk].shape[0] // 2
        previous = add(received[half:], kept[chunk][half:]).astype(jnp.bfloat16)
        kept[chunk] = add(received[:half], kept[chunk][:half]).astype(jnp.bfloat16)
        arrived[chunk] = exchange(previous, orders[chunk][made[chunk]])
        made[chunk] += 1
    return arrived, kept, lists


def node_kernel(held, parts, earlier, reads, mate_list_ref, other_list_ref, *refs):
    summands, refs = refs[:parts], refs[parts:]
    if earlier:
        earlier_ref, refs = refs[0], refs[1:]
    node_in_ref, node_out_ref, gain_ref, scale_ref, to_mate_ref, to_other_ref = refs[:6]
    encoded_refs = refs[6:]
    if parts == 1:
        summed = summands[0][...] * scale_ref[...]
    else:
        pieces = []
        for block in range(held):
            for arrived, kept in zip(summands[: parts // 2], summands[parts // 2 :]):
                cut = arrived.shape[0] // held
                piece = slice(block * cut, (block + 1) * cut)
                pieces.append(add(arrived[piece, :], kept[piece, :]))
        summed = jnp.concatenate(pieces, axis=0) * scale_ref[...]
    rows = summed.shape[0] // held
    hidden = silu(matmul(summed.astype(jnp.bfloat16), node_in_ref[...])).astype(jnp.bfloat16)
    encoded = (summed + gain_ref[...] * normalize(matmul(hidden, node_out_ref[...]))).astype(jnp.bfloat16)
    for out in encoded_refs:
        if earlier:
            ahead = earlier_ref.shape[0] // held
            for block in range(held):
                first = block * (ahead + rows)
                out[first : first + ahead, :] = earlier_ref[block * ahead : (block + 1) * ahead, :]
                out[first + ahead : first + ahead + rows, :] = encoded[block * rows : (block + 1) * rows]
        else:
            out[...] = encoded
    encoded_ref = encoded_refs[0]
    odd = lax.rem(lax.axis_index("space"), 2)
    whole = encoded_ref.shape[0] // held
    for index in range(reads):
        for wanted_ref, first, out in (
            (mate_list_ref, odd * reads, to_mate_ref),
            (other_list_ref, (1 - odd) * reads, to_other_ref),
        ):
            start = pl.multiple_of(wanted_ref[0, first + index] * whole + (whole - rows), 16)
            out[index * rows : (index + 1) * rows, :] = encoded_ref[pl.ds(start, rows), :]


def encode(summands, earlier, scale, node_in, node_out, node_gain, lists, held, copies):
    channels = node_in.shape[0]
    reads = lists[0].shape[1] // 2
    count = sum(summand.shape[0] for summand in summands) // (2 if len(summands) > 1 else 1)
    sent = jax.ShapeDtypeStruct((count // held * reads, channels), jnp.bfloat16)
    total = jax.ShapeDtypeStruct((count + sum(part.shape[0] for part in earlier), channels), jnp.bfloat16)
    return pl.pallas_call(
        functools.partial(node_kernel, held, len(summands), len(earlier), reads),
        in_specs=[SMEM] * 2 + [VMEM] * (len(summands) + len(earlier) + 4),
        out_specs=[VMEM] * (2 + copies),
        out_shape=[sent] * 2 + [total] * copies,
        compiler_params=pltpu.CompilerParams(vmem_limit_bytes=VMEM_BYTES),
        name="node_update",
    )(*lists, *summands, *earlier, node_in, node_out, node_gain.reshape(1, -1), scale.reshape(1, -1))


def operator_kernel(held, reads, splits, dst_ref, src_ref, values_ref, operator_ref, total):
    edges, rows, _ = values_ref.shape
    odd = lax.rem(lax.axis_index("space"), 2)
    total[...] = jnp.zeros_like(total)
    for edge in range(edges):
        side = lax.div(src_ref[edge], held)
        index = lax.rem(src_ref[edge], held)
        across = (odd + lax.div(side, 2) + 1) & 1
        source = jnp.where(side == 1, 2 * reads, across * reads) + index
        first = pl.multiple_of(dst_ref[edge] * rows, rows)
        total[source, pl.ds(first, rows), :] += values_ref[edge].astype(jnp.float32)
    columns = [
        total[source][:, low:high].astype(jnp.bfloat16) for low, high in splits for source in range(2 * reads)
    ]
    columns += [total[source].astype(jnp.bfloat16) for source in range(2 * reads, 2 * reads + held)]
    operator_ref[...] = jnp.concatenate(columns, axis=1)


def mesh_operator(mesh_values, mesh_dst, mesh_src, held, reads, splits):
    rows = mesh_values.shape[1]
    sources = 2 * reads + held
    return pl.pallas_call(
        functools.partial(operator_kernel, held, reads, splits),
        in_specs=[SMEM] * 2 + [VMEM],
        out_specs=VMEM,
        out_shape=jax.ShapeDtypeStruct((held * rows, sources * rows), jnp.bfloat16),
        scratch_shapes=[pltpu.VMEM((sources, held * rows, rows), jnp.float32)],
        compiler_params=pltpu.CompilerParams(vmem_limit_bytes=VMEM_BYTES),
        name="mesh_operator",
    )(mesh_dst, mesh_src, mesh_values)


def process_kernel(operator_ref, own_ref, *refs):
    halos, (proc_in_ref, proc_out_ref, gain_ref, processed_ref) = refs[:-4], refs[-4:]
    sources = jnp.concatenate([halo[...] for halo in halos] + [own_ref[...]], axis=0)
    message = matmul(operator_ref[...], sources)
    hidden = silu(matmul(message.astype(jnp.bfloat16), proc_in_ref[...])).astype(jnp.bfloat16)
    update = gain_ref[...] * normalize(matmul(hidden, proc_out_ref[...]))
    processed_ref[...] = (own_ref[...].astype(jnp.float32) + update).astype(jnp.bfloat16)


def process(operator, own, halos, proc_in, proc_out, proc_gain):
    return pl.pallas_call(
        process_kernel,
        in_specs=[VMEM] * (5 + len(halos)),
        out_specs=VMEM,
        out_shape=jax.ShapeDtypeStruct(own.shape, jnp.bfloat16),
        compiler_params=pltpu.CompilerParams(vmem_limit_bytes=VMEM_BYTES),
        name="process",
    )(operator, own, *halos, proc_in, proc_out, proc_gain.reshape(1, -1))


def lookup(table, wanted):
    matches = wanted[:, None] == jnp.arange(table.shape[0], dtype=jnp.int32)[None, :]
    return jnp.sum(jnp.where(matches, table[None, :], 0), axis=1)


def routed_sum(
    grid_inputs, grid_count, embed_in, embed_out, g2m_values, g2m_src, g2m_dst, mesh_place, partitions
):
    slab_rows = grid_inputs.shape[1]
    edge_count, block_rows, _ = g2m_values.shape
    channels = embed_out.shape[1]
    held = mesh_place.shape[0] // partitions
    capacity = max(1, (edge_count + partitions - 1) // partitions)
    slot_count = partitions * capacity
    hidden = jax.nn.silu(transposed_matmul(grid_inputs, embed_in)).astype(jnp.bfloat16)
    alive = lax.iota(jnp.int32, slab_rows) < grid_count[0]
    latent = jnp.where(alive[:, None], normalize(matmul(hidden, embed_out)), 0.0).astype(jnp.bfloat16)
    positions = lookup(mesh_place, g2m_dst)
    targets = positions // held
    ranking = jnp.sum(jnp.tril(targets[:, None] == targets[None, :], -1), axis=1)
    slot_index = targets * capacity + ranking
    labels = jnp.full((slot_count,), -1, jnp.int32).at[slot_index].set(positions % held)
    sources = latent.reshape(slab_rows // block_rows, block_rows, channels)[g2m_src]
    terms = jnp.einsum("eij,ejd->eid", g2m_values, sources, preferred_element_type=jnp.float32).astype(jnp.bfloat16)
    outgoing = jnp.zeros((slot_count, block_rows, channels), jnp.bfloat16).at[slot_index].set(terms)
    arrived = lax.all_to_all(outgoing, "space", split_axis=0, concat_axis=0, tiled=True)
    arrived_labels = lax.all_to_all(labels, "space", split_axis=0, concat_axis=0, tiled=True)
    selector = (arrived_labels[None, :] == jnp.arange(held, dtype=jnp.int32)[:, None]).astype(jnp.bfloat16)
    return matmul(selector, arrived.reshape(slot_count, -1)).reshape(held * block_rows, channels)


def shards(
    grid_inputs,
    grid_count,
    embed_in,
    embed_out,
    grid_gain,
    g2m_values,
    g2m_src,
    g2m_dst,
    mesh_place,
    node_in,
    node_out,
    node_gain,
    recv_blocks,
    mesh_values,
    mesh_dst,
    mesh_src,
    proc_in,
    proc_out,
    proc_gain,
):
    partitions = lax.axis_size("space")
    edges, rows, _ = g2m_values.shape
    mesh_blocks = mesh_place.shape[0]
    held = mesh_blocks // partitions
    reads = recv_blocks.shape[1] // 2
    mates = [(i, i ^ 1) for i in range(partitions)]
    others = [(i, (i + 1 if i % 2 else i - 1) % partitions) for i in range(partitions)]
    grid_args = (grid_inputs, grid_count, embed_in, embed_out, g2m_values, g2m_src, g2m_dst, mesh_place)
    lists = (lax.ppermute(recv_blocks, "space", mates), lax.ppermute(recv_blocks, "space", others))
    splits = [(0, rows)]
    halos = []
    earlier = []
    if partitions == 1 << (1 + len(ORDERS[0])) and edges % partitions == 0 and edges >= mesh_blocks:
        cuts = [share * rows // sum(SHARES) for share in SHARES]
        sums = slab_sums(*grid_args, partitions, ORDERS, cuts)
        arrived, kept, lists = reduce_chunks(sums[: len(cuts)], sums[len(cuts) :], ORDERS, TURNS, lists)
        if EARLY:
            first = sum(cuts[:EARLY])
            splits = [(0, first), (first, rows)]
            to_mate, to_other, ahead = encode(
                arrived[:EARLY] + kept[:EARLY], [], grid_gain, node_in, node_out, node_gain, lists, held, 1
            )
            halos = [lax.ppermute(to_mate, "space", mates), lax.ppermute(to_other, "space", others)]
            arrived[-1], ahead, halos = lax.optimization_barrier((arrived[-1], ahead, halos))
            earlier = [ahead]
        summands = arrived[EARLY:] + kept[EARLY:]
    else:
        summands = [routed_sum(*grid_args, partitions)]
    operator = mesh_operator(mesh_values, mesh_dst, mesh_src, held, reads, splits)
    to_mate, to_other, encoded, own = encode(
        summands, earlier, grid_gain, node_in, node_out, node_gain, lists, held, 2
    )
    halos += [lax.ppermute(to_mate, "space", mates), lax.ppermute(to_other, "space", others)]
    processed = process(operator, own, halos, proc_in, proc_out, proc_gain)
    return (encoded, processed)


def solution(mesh):
    return jax.shard_map(
        shards,
        mesh=mesh,
        in_specs=(
            P(None, ("groups", "space")),
            P("space"),
            P(),
            P(),
            P(),
            P("space", None, None),
            P("space"),
            P("space"),
            P(),
            P(),
            P(),
            P(),
            P("space", None),
            P("space", None, None),
            P("space"),
            P("space"),
            P(),
            P(),
            P(),
        ),
        out_specs=(P(("groups", "space"), None), P(("groups", "space"), None)),
        check_vma=False,
    )
```

```python
import functools

import jax
import jax.numpy as jnp
from jax import lax
from jax.experimental import pallas as pl
from jax.experimental.pallas import tpu as pltpu
from jax.sharding import PartitionSpec as P

EPSILON = 1e-05
ORDERS = ((1, 2, 3), (2, 1, 3), (3, 1, 2), (1, 2, 3))
SHARES = (2, 2, 2, 2)
TURNS = (2, 0, 1, 3, 0, 1, 2, 3, 0, 1, 2, 3)
EARLY = 1
LISTS_BY = 4
TILE = 1024
UNROLL = 2
VMEM_BYTES = 24 * 1024 * 1024
GRID_VMEM_BYTES = 43 * 1024 * 1024
VMEM = pl.BlockSpec(memory_space=pltpu.VMEM)
SMEM = pl.BlockSpec(memory_space=pltpu.SMEM)
HBM = pl.BlockSpec(memory_space=pltpu.HBM)


def silu(values):
    half = 0.5 * values
    return half + half * jnp.tanh(half)


def normalize(values):
    average = jnp.mean(values, axis=-1, keepdims=True)
    centred = values - average
    variance = jnp.mean(centred * centred, axis=-1, keepdims=True)
    return centred * lax.rsqrt(variance + EPSILON)


def matmul(left, right):
    return jnp.dot(left, right, preferred_element_type=jnp.float32)


def transposed_matmul(left, right):
    return lax.dot_general(left, right, (((0,), (0,)), ((), ())), preferred_element_type=jnp.float32)


def add(left, right):
    return left.astype(jnp.float32) + right.astype(jnp.float32)


def place_of(step, order):
    place = 0
    for bit in order:
        place = place * 2 + ((step >> (bit - 1)) & 1)
    return place


def grid_kernel(
    held,
    capacity,
    orders,
    cuts,
    tile_rows,
    edges,
    table_ref,
    inputs_ref,
    weights_ref,
    values_hbm,
    *refs,
):
    chunks = len(orders)
    outs = (refs[chunks : 2 * chunks], refs[:chunks])
    (
        values_ref,
        latent,
        edge_of,
        filled,
        crowded_of,
        crowded,
        load_sem,
    ) = refs[2 * chunks :]
    rows = values_ref.shape[1]
    slots = edges // capacity
    pairs = slots // 2
    load = pltpu.make_async_copy(values_hbm, values_ref, load_sem)
    load.start()

    me = lax.axis_index("space")

    def clear(bin_, carry):
        filled[bin_] = 0
        for index in range(2):
            edge_of[bin_ * capacity + index] = 0
        return carry

    lax.fori_loop(0, slots * held, clear, 0)
    crowded[0] = 0

    def sort(edge):
        bin_ = table_ref[2 * edges + table_ref[edges + edge]] ^ (me * held)
        count = filled[bin_]
        edge_of[bin_ * capacity + count] = edge
        filled[bin_] = count + 1
        seen = crowded[0]
        crowded_of[seen] = bin_
        crowded[0] = seen + (count == 2).astype(jnp.int32)


    channels = latent.shape[1]
    alive = table_ref[table_ref.shape[0] - 1]
    tiles = latent.shape[0] // tile_rows
    sorted_each = edges // tiles

    def embed(tile, carry):
        for index in range(sorted_each):
            sort(tile * sorted_each + index)
        first = pl.multiple_of(tile * tile_rows, tile_rows)
        columns = inputs_ref[:, pl.ds(first, tile_rows)]
        hidden = silu(transposed_matmul(columns, weights_ref[channels:, :])).astype(jnp.bfloat16)
        normal = normalize(matmul(hidden, weights_ref[:channels, :]))
        row = first + lax.broadcasted_iota(jnp.int32, (tile_rows, 1), 0)
        latent[pl.ds(first, tile_rows), :] = jnp.where(row < alive, normal, 0.0).astype(jnp.bfloat16)
        return carry

    lax.fori_loop(0, tiles, embed, 0, unroll=True)
    for edge in range(tiles * sorted_each, edges):
        sort(edge)
    load.wait()

    def product(bin_, first, count):
        operator = []
        sources = []
        for index in range(first, first + 2):
            edge = jnp.where(count > index, edge_of[bin_ * capacity + index], 0)
            values = values_ref[edge]
            operator.append(jnp.where(count > index, values, jnp.zeros_like(values)))
            start = pl.multiple_of(table_ref[edge] * rows, rows)
            sources.append(latent[pl.ds(start, rows), :])
        return matmul(jnp.concatenate(operator, axis=1), jnp.concatenate(sources, axis=0))

    def store(pair, side, block, summed):
        top = 0
        for out, order, cut in zip(outs[side], orders, cuts):
            first = pl.multiple_of((place_of(pair, order) * held + block) * cut, 16)
            out[pl.ds(first, cut), :] = summed[top : top + cut].astype(jnp.bfloat16)
            top += cut

    def multiply(turn, carry):
        for pair in (2 * turn, 2 * turn + 1):
            for side in range(2):
                for block in range(held):
                    bin_ = (2 * pair + side) * held + block
                    store(pair, side, block, product(bin_, 0, filled[bin_]))

        return carry

    lax.fori_loop(0, pairs // 2, multiply, 0, unroll=UNROLL)

    def revisit(index, carry):
        bin_ = crowded_of[index]
        count = filled[bin_]
        summed = product(bin_, 0, count)
        for first in range(2, capacity, 2):
            summed = summed + product(bin_, first, count)
        pair = lax.div(bin_, 2 * held)
        side = lax.rem(lax.div(bin_, held), 2)
        for each in range(2):

            @pl.when(side == each)
            def _(each=each):
                store(pair, each, lax.rem(bin_, held), summed)

        return carry

    lax.fori_loop(0, crowded[0], revisit, 0)


def slab_sums(
    grid_inputs,
    grid_count,
    embed_in,
    embed_out,
    g2m_values,
    g2m_src,
    g2m_dst,
    mesh_place,
    partitions,
    orders,
    cuts,
):
    slab_rows = grid_inputs.shape[1]
    channels = embed_out.shape[1]
    edges, rows, _ = g2m_values.shape
    held = mesh_place.shape[0] // partitions
    capacity = edges // partitions
    pairs = partitions // 2
    shapes = [jax.ShapeDtypeStruct((pairs * held * cut, channels), jnp.bfloat16) for cut in cuts]
    return pl.pallas_call(
        functools.partial(grid_kernel, held, capacity, orders, cuts, min(TILE, slab_rows), edges),
        in_specs=[SMEM] + [VMEM] * 2 + [HBM],
        out_specs=[VMEM] * (2 * len(cuts)),
        out_shape=shapes * 2,
        scratch_shapes=[
            pltpu.VMEM(g2m_values.shape, jnp.bfloat16),
            pltpu.VMEM((slab_rows, channels), jnp.bfloat16),
            pltpu.SMEM((partitions * held * capacity,), jnp.int32),
            pltpu.SMEM((partitions * held,), jnp.int32),
            pltpu.SMEM((partitions * held + 1,), jnp.int32),
            pltpu.SMEM((1,), jnp.int32),
            pltpu.SemaphoreType.DMA,
        ],
        compiler_params=pltpu.CompilerParams(vmem_limit_bytes=GRID_VMEM_BYTES),
        name="grid_to_mesh",
    )(
        jnp.concatenate([g2m_src, g2m_dst, mesh_place, grid_count]),
        grid_inputs,
        jnp.concatenate([embed_out, embed_in]),
        g2m_values,
    )


def exchange(cells, bit):
    count = lax.axis_size("space")
    return lax.ppermute(cells, "space", [(i, i ^ (1 << bit)) for i in range(count)])


def reduce_chunks(mates, owns, orders, turns, lists):
    arrived = [exchange(mate, 0) for mate in mates]
    kept = list(owns)
    made = [0] * len(orders)
    for turn, chunk in enumerate(turns):
        received = arrived[chunk]
        if turn == LISTS_BY:
            received, _, lists = lax.optimization_barrier((received, previous, lists))
        elif turn > 0:
            received, _ = lax.optimization_barrier((received, previous))
        half = kept[chunk].shape[0] // 2
        previous = add(received[half:], kept[chunk][half:]).astype(jnp.bfloat16)
        kept[chunk] = add(received[:half], kept[chunk][:half]).astype(jnp.bfloat16)
        arrived[chunk] = exchange(previous, orders[chunk][made[chunk]])
        made[chunk] += 1
    return arrived, kept, lists


def node_kernel(held, parts, earlier, reads, mate_list_ref, other_list_ref, *refs):
    summands, refs = refs[:parts], refs[parts:]
    if earlier:
        earlier_ref, refs = refs[0], refs[1:]
    node_in_ref, node_out_ref, gain_ref, scale_ref, to_mate_ref, to_other_ref = refs[:6]
    encoded_refs = refs[6:]
    if parts == 1:
        summed = summands[0][...] * scale_ref[...]
    else:
        pieces = []
        for block in range(held):
            for arrived, kept in zip(summands[: parts // 2], summands[parts // 2 :]):
                cut = arrived.shape[0] // held
                piece = slice(block * cut, (block + 1) * cut)
                pieces.append(add(arrived[piece, :], kept[piece, :]))
        summed = jnp.concatenate(pieces, axis=0) * scale_ref[...]
    rows = summed.shape[0] // held
    hidden = silu(matmul(summed.astype(jnp.bfloat16), node_in_ref[...])).astype(jnp.bfloat16)
    encoded = (summed + gain_ref[...] * normalize(matmul(hidden, node_out_ref[...]))).astype(jnp.bfloat16)
    for out in encoded_refs:
        if earlier:
            ahead = earlier_ref.shape[0] // held
            for block in range(held):
                first = block * (ahead + rows)
                out[first : first + ahead, :] = earlier_ref[block * ahead : (block + 1) * ahead, :]
                out[first + ahead : first + ahead + rows, :] = encoded[block * rows : (block + 1) * rows]
        else:
            out[...] = encoded
    encoded_ref = encoded_refs[0]
    odd = lax.rem(lax.axis_index("space"), 2)
    whole = encoded_ref.shape[0] // held
    for index in range(reads):
        for wanted_ref, first, out in (
            (mate_list_ref, odd * reads, to_mate_ref),
            (other_list_ref, (1 - odd) * reads, to_other_ref),
        ):
            start = pl.multiple_of(wanted_ref[0, first + index] * whole + (whole - rows), 16)
            out[index * rows : (index + 1) * rows, :] = encoded_ref[pl.ds(start, rows), :]


def encode(summands, earlier, scale, node_in, node_out, node_gain, lists, held, copies):
    channels = node_in.shape[0]
    reads = lists[0].shape[1] // 2
    count = sum(summand.shape[0] for summand in summands) // (2 if len(summands) > 1 else 1)
    sent = jax.ShapeDtypeStruct((count // held * reads, channels), jnp.bfloat16)
    total = jax.ShapeDtypeStruct((count + sum(part.shape[0] for part in earlier), channels), jnp.bfloat16)
    return pl.pallas_call(
        functools.partial(node_kernel, held, len(summands), len(earlier), reads),
        in_specs=[SMEM] * 2 + [VMEM] * (len(summands) + len(earlier) + 4),
        out_specs=[VMEM] * (2 + copies),
        out_shape=[sent] * 2 + [total] * copies,
        compiler_params=pltpu.CompilerParams(vmem_limit_bytes=VMEM_BYTES),
        name="node_update",
    )(*lists, *summands, *earlier, node_in, node_out, node_gain.reshape(1, -1), scale.reshape(1, -1))


def operator_kernel(held, reads, splits, dst_ref, src_ref, values_ref, operator_ref, total):
    edges, rows, _ = values_ref.shape
    odd = lax.rem(lax.axis_index("space"), 2)
    total[...] = jnp.zeros_like(total)
    for edge in range(edges):
        side = lax.div(src_ref[edge], held)
        index = lax.rem(src_ref[edge], held)
        across = (odd + lax.div(side, 2) + 1) & 1
        source = jnp.where(side == 1, 2 * reads, across * reads) + index
        first = pl.multiple_of(dst_ref[edge] * rows, rows)
        total[source, pl.ds(first, rows), :] += values_ref[edge].astype(jnp.float32)
    columns = [
        total[source][:, low:high].astype(jnp.bfloat16) for low, high in splits for source in range(2 * reads)
    ]
    columns += [total[source].astype(jnp.bfloat16) for source in range(2 * reads, 2 * reads + held)]
    operator_ref[...] = jnp.concatenate(columns, axis=1)


def mesh_operator(mesh_values, mesh_dst, mesh_src, held, reads, splits):
    rows = mesh_values.shape[1]
    sources = 2 * reads + held
    return pl.pallas_call(
        functools.partial(operator_kernel, held, reads, splits),
        in_specs=[SMEM] * 2 + [VMEM],
        out_specs=VMEM,
        out_shape=jax.ShapeDtypeStruct((held * rows, sources * rows), jnp.bfloat16),
        scratch_shapes=[pltpu.VMEM((sources, held * rows, rows), jnp.float32)],
        compiler_params=pltpu.CompilerParams(vmem_limit_bytes=VMEM_BYTES),
        name="mesh_operator",
    )(mesh_dst, mesh_src, mesh_values)


def process_kernel(operator_ref, own_ref, *refs):
    halos, (proc_in_ref, proc_out_ref, gain_ref, processed_ref) = refs[:-4], refs[-4:]
    sources = jnp.concatenate([halo[...] for halo in halos] + [own_ref[...]], axis=0)
    message = matmul(operator_ref[...], sources)
    hidden = silu(matmul(message.astype(jnp.bfloat16), proc_in_ref[...])).astype(jnp.bfloat16)
    update = gain_ref[...] * normalize(matmul(hidden, proc_out_ref[...]))
    processed_ref[...] = (own_ref[...].astype(jnp.float32) + update).astype(jnp.bfloat16)


def process(operator, own, halos, proc_in, proc_out, proc_gain):
    return pl.pallas_call(
        process_kernel,
        in_specs=[VMEM] * (5 + len(halos)),
        out_specs=VMEM,
        out_shape=jax.ShapeDtypeStruct(own.shape, jnp.bfloat16),
        compiler_params=pltpu.CompilerParams(vmem_limit_bytes=VMEM_BYTES),
        name="process",
    )(operator, own, *halos, proc_in, proc_out, proc_gain.reshape(1, -1))


def lookup(table, wanted):
    matches = wanted[:, None] == jnp.arange(table.shape[0], dtype=jnp.int32)[None, :]
    return jnp.sum(jnp.where(matches, table[None, :], 0), axis=1)


def routed_sum(
    grid_inputs, grid_count, embed_in, embed_out, g2m_values, g2m_src, g2m_dst, mesh_place, partitions
):
    slab_rows = grid_inputs.shape[1]
    edge_count, block_rows, _ = g2m_values.shape
    channels = embed_out.shape[1]
    held = mesh_place.shape[0] // partitions
    capacity = max(1, (edge_count + partitions - 1) // partitions)
    slot_count = partitions * capacity
    hidden = jax.nn.silu(transposed_matmul(grid_inputs, embed_in)).astype(jnp.bfloat16)
    alive = lax.iota(jnp.int32, slab_rows) < grid_count[0]
    latent = jnp.where(alive[:, None], normalize(matmul(hidden, embed_out)), 0.0).astype(jnp.bfloat16)
    positions = lookup(mesh_place, g2m_dst)
    targets = positions // held
    ranking = jnp.sum(jnp.tril(targets[:, None] == targets[None, :], -1), axis=1)
    slot_index = targets * capacity + ranking
    labels = jnp.full((slot_count,), -1, jnp.int32).at[slot_index].set(positions % held)
    sources = latent.reshape(slab_rows // block_rows, block_rows, channels)[g2m_src]
    terms = jnp.einsum("eij,ejd->eid", g2m_values, sources, preferred_element_type=jnp.float32).astype(jnp.bfloat16)
    outgoing = jnp.zeros((slot_count, block_rows, channels), jnp.bfloat16).at[slot_index].set(terms)
    arrived = lax.all_to_all(outgoing, "space", split_axis=0, concat_axis=0, tiled=True)
    arrived_labels = lax.all_to_all(labels, "space", split_axis=0, concat_axis=0, tiled=True)
    selector = (arrived_labels[None, :] == jnp.arange(held, dtype=jnp.int32)[:, None]).astype(jnp.bfloat16)
    return matmul(selector, arrived.reshape(slot_count, -1)).reshape(held * block_rows, channels)


def shards(
    grid_inputs,
    grid_count,
    embed_in,
    embed_out,
    grid_gain,
    g2m_values,
    g2m_src,
    g2m_dst,
    mesh_place,
    node_in,
    node_out,
    node_gain,
    recv_blocks,
    mesh_values,
    mesh_dst,
    mesh_src,
    proc_in,
    proc_out,
    proc_gain,
):
    partitions = lax.axis_size("space")
    edges, rows, _ = g2m_values.shape
    mesh_blocks = mesh_place.shape[0]
    held = mesh_blocks // partitions
    reads = recv_blocks.shape[1] // 2
    mates = [(i, i ^ 1) for i in range(partitions)]
    others = [(i, (i + 1 if i % 2 else i - 1) % partitions) for i in range(partitions)]
    grid_args = (grid_inputs, grid_count, embed_in, embed_out, g2m_values, g2m_src, g2m_dst, mesh_place)
    lists = (lax.ppermute(recv_blocks, "space", mates), lax.ppermute(recv_blocks, "space", others))
    splits = [(0, rows)]
    halos = []
    earlier = []
    if partitions == 1 << (1 + len(ORDERS[0])) and edges % partitions == 0 and edges >= mesh_blocks:
        cuts = [share * rows // sum(SHARES) for share in SHARES]
        sums = slab_sums(*grid_args, partitions, ORDERS, cuts)
        arrived, kept, lists = reduce_chunks(sums[: len(cuts)], sums[len(cuts) :], ORDERS, TURNS, lists)
        if EARLY:
            first = sum(cuts[:EARLY])
            splits = [(0, first), (first, rows)]
            to_mate, to_other, ahead = encode(
                arrived[:EARLY] + kept[:EARLY], [], grid_gain, node_in, node_out, node_gain, lists, held, 1
            )
            halos = [lax.ppermute(to_mate, "space", mates), lax.ppermute(to_other, "space", others)]
            arrived[-1], ahead, halos = lax.optimization_barrier((arrived[-1], ahead, halos))
            earlier = [ahead]
        summands = arrived[EARLY:] + kept[EARLY:]
    else:
        summands = [routed_sum(*grid_args, partitions)]
    operator = mesh_operator(mesh_values, mesh_dst, mesh_src, held, reads, splits)
    to_mate, to_other, encoded, own = encode(
        summands, earlier, grid_gain, node_in, node_out, node_gain, lists, held, 2
    )
    halos += [lax.ppermute(to_mate, "space", mates), lax.ppermute(to_other, "space", others)]
    processed = process(operator, own, halos, proc_in, proc_out, proc_gain)
    return (encoded, processed)


def solution(mesh):
    return jax.shard_map(
        shards,
        mesh=mesh,
        in_specs=(
            P(None, ("groups", "space")),
            P("space"),
            P(),
            P(),
            P(),
            P("space", None, None),
            P("space"),
            P("space"),
            P(),
            P(),
            P(),
            P(),
            P("space", None),
            P("space", None, None),
            P("space"),
            P("space"),
            P(),
            P(),
            P(),
        ),
        out_specs=(P(("groups", "space"), None), P(("groups", "space"), None)),
        check_vma=False,
    )
```

```python
import functools

import jax
import jax.numpy as jnp
from jax import lax
from jax.experimental import pallas as pl
from jax.experimental.pallas import tpu as pltpu
from jax.sharding import PartitionSpec as P

EPSILON = 1e-05
ORDERS = ((1, 2, 3), (2, 1, 3), (3, 1, 2), (1, 2, 3))
SHARES = (2, 2, 2, 2)
TURNS = (2, 0, 1, 3, 0, 1, 2, 3, 0, 1, 2, 3)
EARLY = 1
LISTS_BY = 4
TILE = 2048
UNROLL = 2
VMEM_BYTES = 24 * 1024 * 1024
GRID_VMEM_BYTES = 43 * 1024 * 1024
VMEM = pl.BlockSpec(memory_space=pltpu.VMEM)
SMEM = pl.BlockSpec(memory_space=pltpu.SMEM)
HBM = pl.BlockSpec(memory_space=pltpu.HBM)


def silu(values):
    half = 0.5 * values
    return half + half * jnp.tanh(half)


def normalize(values):
    average = jnp.mean(values, axis=-1, keepdims=True)
    centred = values - average
    variance = jnp.mean(centred * centred, axis=-1, keepdims=True)
    return centred * lax.rsqrt(variance + EPSILON)


def matmul(left, right):
    return jnp.dot(left, right, preferred_element_type=jnp.float32)


def transposed_matmul(left, right):
    return lax.dot_general(left, right, (((0,), (0,)), ((), ())), preferred_element_type=jnp.float32)


def add(left, right):
    return left.astype(jnp.float32) + right.astype(jnp.float32)


def place_of(step, order):
    place = 0
    for bit in order:
        place = place * 2 + ((step >> (bit - 1)) & 1)
    return place


def grid_kernel(
    held,
    capacity,
    orders,
    cuts,
    tile_rows,
    edges,
    table_ref,
    inputs_ref,
    weights_ref,
    values_hbm,
    *refs,
):
    chunks = len(orders)
    outs = (refs[chunks : 2 * chunks], refs[:chunks])
    (
        values_ref,
        latent,
        edge_of,
        filled,
        crowded_of,
        crowded,
        load_sem,
    ) = refs[2 * chunks :]
    rows = values_ref.shape[1]
    slots = edges // capacity
    pairs = slots // 2
    load = pltpu.make_async_copy(values_hbm, values_ref, load_sem)
    load.start()

    me = lax.axis_index("space")

    def clear(bin_, carry):
        filled[bin_] = 0
        for index in range(2):
            edge_of[bin_ * capacity + index] = 0
        return carry

    lax.fori_loop(0, slots * held, clear, 0)
    crowded[0] = 0

    def sort(edge):
        bin_ = table_ref[2 * edges + table_ref[edges + edge]] ^ (me * held)
        count = filled[bin_]
        edge_of[bin_ * capacity + count] = edge
        filled[bin_] = count + 1
        seen = crowded[0]
        crowded_of[seen] = bin_
        crowded[0] = seen + (count == 2).astype(jnp.int32)


    channels = latent.shape[1]
    alive = table_ref[table_ref.shape[0] - 1]
    tiles = latent.shape[0] // tile_rows
    sorted_each = edges // tiles

    def embed(tile, carry):
        for index in range(sorted_each):
            sort(tile * sorted_each + index)
        first = pl.multiple_of(tile * tile_rows, tile_rows)
        columns = inputs_ref[:, pl.ds(first, tile_rows)]
        hidden = silu(transposed_matmul(columns, weights_ref[channels:, :])).astype(jnp.bfloat16)
        normal = normalize(matmul(hidden, weights_ref[:channels, :]))
        row = first + lax.broadcasted_iota(jnp.int32, (tile_rows, 1), 0)
        latent[pl.ds(first, tile_rows), :] = jnp.where(row < alive, normal, 0.0).astype(jnp.bfloat16)
        return carry

    lax.fori_loop(0, tiles, embed, 0, unroll=True)
    for edge in range(tiles * sorted_each, edges):
        sort(edge)
    load.wait()

    def product(bin_, first, count):
        operator = []
        sources = []
        for index in range(first, first + 2):
            edge = jnp.where(count > index, edge_of[bin_ * capacity + index], 0)
            values = values_ref[edge]
            operator.append(jnp.where(count > index, values, jnp.zeros_like(values)))
            start = pl.multiple_of(table_ref[edge] * rows, rows)
            sources.append(latent[pl.ds(start, rows), :])
        return matmul(jnp.concatenate(operator, axis=1), jnp.concatenate(sources, axis=0))

    def store(pair, side, block, summed):
        top = 0
        for out, order, cut in zip(outs[side], orders, cuts):
            first = pl.multiple_of((place_of(pair, order) * held + block) * cut, 16)
            out[pl.ds(first, cut), :] = summed[top : top + cut].astype(jnp.bfloat16)
            top += cut

    def multiply(turn, carry):
        for pair in (2 * turn, 2 * turn + 1):
            for side in range(2):
                for block in range(held):
                    bin_ = (2 * pair + side) * held + block
                    store(pair, side, block, product(bin_, 0, filled[bin_]))

        return carry

    lax.fori_loop(0, pairs // 2, multiply, 0, unroll=UNROLL)

    def revisit(index, carry):
        bin_ = crowded_of[index]
        count = filled[bin_]
        summed = product(bin_, 0, count)
        for first in range(2, capacity, 2):
            summed = summed + product(bin_, first, count)
        pair = lax.div(bin_, 2 * held)
        side = lax.rem(lax.div(bin_, held), 2)
        for each in range(2):

            @pl.when(side == each)
            def _(each=each):
                store(pair, each, lax.rem(bin_, held), summed)

        return carry

    lax.fori_loop(0, crowded[0], revisit, 0)


def slab_sums(
    grid_inputs,
    grid_count,
    embed_in,
    embed_out,
    g2m_values,
    g2m_src,
    g2m_dst,
    mesh_place,
    partitions,
    orders,
    cuts,
):
    slab_rows = grid_inputs.shape[1]
    channels = embed_out.shape[1]
    edges, rows, _ = g2m_values.shape
    held = mesh_place.shape[0] // partitions
    capacity = edges // partitions
    pairs = partitions // 2
    shapes = [jax.ShapeDtypeStruct((pairs * held * cut, channels), jnp.bfloat16) for cut in cuts]
    return pl.pallas_call(
        functools.partial(grid_kernel, held, capacity, orders, cuts, min(TILE, slab_rows), edges),
        in_specs=[SMEM] + [VMEM] * 2 + [HBM],
        out_specs=[VMEM] * (2 * len(cuts)),
        out_shape=shapes * 2,
        scratch_shapes=[
            pltpu.VMEM(g2m_values.shape, jnp.bfloat16),
            pltpu.VMEM((slab_rows, channels), jnp.bfloat16),
            pltpu.SMEM((partitions * held * capacity,), jnp.int32),
            pltpu.SMEM((partitions * held,), jnp.int32),
            pltpu.SMEM((partitions * held + 1,), jnp.int32),
            pltpu.SMEM((1,), jnp.int32),
            pltpu.SemaphoreType.DMA,
        ],
        compiler_params=pltpu.CompilerParams(vmem_limit_bytes=GRID_VMEM_BYTES),
        name="grid_to_mesh",
    )(
        jnp.concatenate([g2m_src, g2m_dst, mesh_place, grid_count]),
        grid_inputs,
        jnp.concatenate([embed_out, embed_in]),
        g2m_values,
    )


def exchange(cells, bit):
    count = lax.axis_size("space")
    return lax.ppermute(cells, "space", [(i, i ^ (1 << bit)) for i in range(count)])


def reduce_chunks(mates, owns, orders, turns, lists):
    arrived = [exchange(mate, 0) for mate in mates]
    kept = list(owns)
    made = [0] * len(orders)
    for turn, chunk in enumerate(turns):
        received = arrived[chunk]
        if turn == LISTS_BY:
            received, _, lists = lax.optimization_barrier((received, previous, lists))
        elif turn > 0:
            received, _ = lax.optimization_barrier((received, previous))
        half = kept[chunk].shape[0] // 2
        previous = add(received[half:], kept[chunk][half:]).astype(jnp.bfloat16)
        kept[chunk] = add(received[:half], kept[chunk][:half]).astype(jnp.bfloat16)
        arrived[chunk] = exchange(previous, orders[chunk][made[chunk]])
        made[chunk] += 1
    return arrived, kept, lists


def node_kernel(held, parts, earlier, reads, mate_list_ref, other_list_ref, *refs):
    summands, refs = refs[:parts], refs[parts:]
    if earlier:
        earlier_ref, refs = refs[0], refs[1:]
    node_in_ref, node_out_ref, gain_ref, scale_ref, to_mate_ref, to_other_ref = refs[:6]
    encoded_refs = refs[6:]
    if parts == 1:
        summed = summands[0][...] * scale_ref[...]
    else:
        pieces = []
        for block in range(held):
            for arrived, kept in zip(summands[: parts // 2], summands[parts // 2 :]):
                cut = arrived.shape[0] // held
                piece = slice(block * cut, (block + 1) * cut)
                pieces.append(add(arrived[piece, :], kept[piece, :]))
        summed = jnp.concatenate(pieces, axis=0) * scale_ref[...]
    rows = summed.shape[0] // held
    hidden = silu(matmul(summed.astype(jnp.bfloat16), node_in_ref[...])).astype(jnp.bfloat16)
    encoded = (summed + gain_ref[...] * normalize(matmul(hidden, node_out_ref[...]))).astype(jnp.bfloat16)
    for out in encoded_refs:
        if earlier:
            ahead = earlier_ref.shape[0] // held
            for block in range(held):
                first = block * (ahead + rows)
                out[first : first + ahead, :] = earlier_ref[block * ahead : (block + 1) * ahead, :]
                out[first + ahead : first + ahead + rows, :] = encoded[block * rows : (block + 1) * rows]
        else:
            out[...] = encoded
    encoded_ref = encoded_refs[0]
    odd = lax.rem(lax.axis_index("space"), 2)
    whole = encoded_ref.shape[0] // held
    for index in range(reads):
        for wanted_ref, first, out in (
            (mate_list_ref, odd * reads, to_mate_ref),
            (other_list_ref, (1 - odd) * reads, to_other_ref),
        ):
            start = pl.multiple_of(wanted_ref[0, first + index] * whole + (whole - rows), 16)
            out[index * rows : (index + 1) * rows, :] = encoded_ref[pl.ds(start, rows), :]


def encode(summands, earlier, scale, node_in, node_out, node_gain, lists, held, copies):
    channels = node_in.shape[0]
    reads = lists[0].shape[1] // 2
    count = sum(summand.shape[0] for summand in summands) // (2 if len(summands) > 1 else 1)
    sent = jax.ShapeDtypeStruct((count // held * reads, channels), jnp.bfloat16)
    total = jax.ShapeDtypeStruct((count + sum(part.shape[0] for part in earlier), channels), jnp.bfloat16)
    return pl.pallas_call(
        functools.partial(node_kernel, held, len(summands), len(earlier), reads),
        in_specs=[SMEM] * 2 + [VMEM] * (len(summands) + len(earlier) + 4),
        out_specs=[VMEM] * (2 + copies),
        out_shape=[sent] * 2 + [total] * copies,
        compiler_params=pltpu.CompilerParams(vmem_limit_bytes=VMEM_BYTES),
        name="node_update",
    )(*lists, *summands, *earlier, node_in, node_out, node_gain.reshape(1, -1), scale.reshape(1, -1))


def operator_kernel(held, reads, splits, dst_ref, src_ref, values_ref, operator_ref, total):
    edges, rows, _ = values_ref.shape
    odd = lax.rem(lax.axis_index("space"), 2)
    total[...] = jnp.zeros_like(total)
    for edge in range(edges):
        side = lax.div(src_ref[edge], held)
        index = lax.rem(src_ref[edge], held)
        across = (odd + lax.div(side, 2) + 1) & 1
        source = jnp.where(side == 1, 2 * reads, across * reads) + index
        first = pl.multiple_of(dst_ref[edge] * rows, rows)
        total[source, pl.ds(first, rows), :] += values_ref[edge].astype(jnp.float32)
    columns = [
        total[source][:, low:high].astype(jnp.bfloat16) for low, high in splits for source in range(2 * reads)
    ]
    columns += [total[source].astype(jnp.bfloat16) for source in range(2 * reads, 2 * reads + held)]
    operator_ref[...] = jnp.concatenate(columns, axis=1)


def mesh_operator(mesh_values, mesh_dst, mesh_src, held, reads, splits):
    rows = mesh_values.shape[1]
    sources = 2 * reads + held
    return pl.pallas_call(
        functools.partial(operator_kernel, held, reads, splits),
        in_specs=[SMEM] * 2 + [VMEM],
        out_specs=VMEM,
        out_shape=jax.ShapeDtypeStruct((held * rows, sources * rows), jnp.bfloat16),
        scratch_shapes=[pltpu.VMEM((sources, held * rows, rows), jnp.float32)],
        compiler_params=pltpu.CompilerParams(vmem_limit_bytes=VMEM_BYTES),
        name="mesh_operator",
    )(mesh_dst, mesh_src, mesh_values)


def process_kernel(operator_ref, own_ref, *refs):
    halos, (proc_in_ref, proc_out_ref, gain_ref, processed_ref) = refs[:-4], refs[-4:]
    sources = jnp.concatenate([halo[...] for halo in halos] + [own_ref[...]], axis=0)
    message = matmul(operator_ref[...], sources)
    hidden = silu(matmul(message.astype(jnp.bfloat16), proc_in_ref[...])).astype(jnp.bfloat16)
    update = gain_ref[...] * normalize(matmul(hidden, proc_out_ref[...]))
    processed_ref[...] = (own_ref[...].astype(jnp.float32) + update).astype(jnp.bfloat16)


def process(operator, own, halos, proc_in, proc_out, proc_gain):
    return pl.pallas_call(
        process_kernel,
        in_specs=[VMEM] * (5 + len(halos)),
        out_specs=VMEM,
        out_shape=jax.ShapeDtypeStruct(own.shape, jnp.bfloat16),
        compiler_params=pltpu.CompilerParams(vmem_limit_bytes=VMEM_BYTES),
        name="process",
    )(operator, own, *halos, proc_in, proc_out, proc_gain.reshape(1, -1))


def lookup(table, wanted):
    matches = wanted[:, None] == jnp.arange(table.shape[0], dtype=jnp.int32)[None, :]
    return jnp.sum(jnp.where(matches, table[None, :], 0), axis=1)


def routed_sum(
    grid_inputs, grid_count, embed_in, embed_out, g2m_values, g2m_src, g2m_dst, mesh_place, partitions
):
    slab_rows = grid_inputs.shape[1]
    edge_count, block_rows, _ = g2m_values.shape
    channels = embed_out.shape[1]
    held = mesh_place.shape[0] // partitions
    capacity = max(1, (edge_count + partitions - 1) // partitions)
    slot_count = partitions * capacity
    hidden = jax.nn.silu(transposed_matmul(grid_inputs, embed_in)).astype(jnp.bfloat16)
    alive = lax.iota(jnp.int32, slab_rows) < grid_count[0]
    latent = jnp.where(alive[:, None], normalize(matmul(hidden, embed_out)), 0.0).astype(jnp.bfloat16)
    positions = lookup(mesh_place, g2m_dst)
    targets = positions // held
    ranking = jnp.sum(jnp.tril(targets[:, None] == targets[None, :], -1), axis=1)
    slot_index = targets * capacity + ranking
    labels = jnp.full((slot_count,), -1, jnp.int32).at[slot_index].set(positions % held)
    sources = latent.reshape(slab_rows // block_rows, block_rows, channels)[g2m_src]
    terms = jnp.einsum("eij,ejd->eid", g2m_values, sources, preferred_element_type=jnp.float32).astype(jnp.bfloat16)
    outgoing = jnp.zeros((slot_count, block_rows, channels), jnp.bfloat16).at[slot_index].set(terms)
    arrived = lax.all_to_all(outgoing, "space", split_axis=0, concat_axis=0, tiled=True)
    arrived_labels = lax.all_to_all(labels, "space", split_axis=0, concat_axis=0, tiled=True)
    selector = (arrived_labels[None, :] == jnp.arange(held, dtype=jnp.int32)[:, None]).astype(jnp.bfloat16)
    return matmul(selector, arrived.reshape(slot_count, -1)).reshape(held * block_rows, channels)


def shards(
    grid_inputs,
    grid_count,
    embed_in,
    embed_out,
    grid_gain,
    g2m_values,
    g2m_src,
    g2m_dst,
    mesh_place,
    node_in,
    node_out,
    node_gain,
    recv_blocks,
    mesh_values,
    mesh_dst,
    mesh_src,
    proc_in,
    proc_out,
    proc_gain,
):
    partitions = lax.axis_size("space")
    edges, rows, _ = g2m_values.shape
    mesh_blocks = mesh_place.shape[0]
    held = mesh_blocks // partitions
    reads = recv_blocks.shape[1] // 2
    mates = [(i, i ^ 1) for i in range(partitions)]
    others = [(i, (i + 1 if i % 2 else i - 1) % partitions) for i in range(partitions)]
    grid_args = (grid_inputs, grid_count, embed_in, embed_out, g2m_values, g2m_src, g2m_dst, mesh_place)
    lists = (lax.ppermute(recv_blocks, "space", mates), lax.ppermute(recv_blocks, "space", others))
    splits = [(0, rows)]
    halos = []
    earlier = []
    if partitions == 1 << (1 + len(ORDERS[0])) and edges % partitions == 0 and edges >= mesh_blocks:
        cuts = [share * rows // sum(SHARES) for share in SHARES]
        sums = slab_sums(*grid_args, partitions, ORDERS, cuts)
        arrived, kept, lists = reduce_chunks(sums[: len(cuts)], sums[len(cuts) :], ORDERS, TURNS, lists)
        if EARLY:
            first = sum(cuts[:EARLY])
            splits = [(0, first), (first, rows)]
            to_mate, to_other, ahead = encode(
                arrived[:EARLY] + kept[:EARLY], [], grid_gain, node_in, node_out, node_gain, lists, held, 1
            )
            halos = [lax.ppermute(to_mate, "space", mates), lax.ppermute(to_other, "space", others)]
            arrived[-1], ahead, halos = lax.optimization_barrier((arrived[-1], ahead, halos))
            earlier = [ahead]
        summands = arrived[EARLY:] + kept[EARLY:]
    else:
        summands = [routed_sum(*grid_args, partitions)]
    operator = mesh_operator(mesh_values, mesh_dst, mesh_src, held, reads, splits)
    to_mate, to_other, encoded, own = encode(
        summands, earlier, grid_gain, node_in, node_out, node_gain, lists, held, 2
    )
    halos += [lax.ppermute(to_mate, "space", mates), lax.ppermute(to_other, "space", others)]
    processed = process(operator, own, halos, proc_in, proc_out, proc_gain)
    return (encoded, processed)


def solution(mesh):
    return jax.shard_map(
        shards,
        mesh=mesh,
        in_specs=(
            P(None, ("groups", "space")),
            P("space"),
            P(),
            P(),
            P(),
            P("space", None, None),
            P("space"),
            P("space"),
            P(),
            P(),
            P(),
            P(),
            P("space", None),
            P("space", None, None),
            P("space"),
            P("space"),
            P(),
            P(),
            P(),
        ),
        out_specs=(P(("groups", "space"), None), P(("groups", "space"), None)),
        check_vma=False,
    )
```
